32 devices in a mesh: groups: 2 (over y), seq: 8 (over z, x), head: 2 (over core).
Axes of the slice: x: 2, y: 2, z: 4, core: 2. Of those that a mesh axis runs over, the one named last changes fastest.
Arguments:
- cache_pool: bfloat16 [768, 128, 576], P(('groups', 'seq')), parts along dimension 0, may hold values from -6 to 6, as said below
- page_table: int32 [4, 128], P('groups'), parts along dimension 0, may hold values from -1 to 383, as said below
- prompt_len: int32 [4], P('groups'), parts along dimension 0, may hold values from 2048 to 16384, as said below
- host_samples: int32 [32], P(('groups', 'seq')), parts along dimension 0, may hold values from 0 to 15, as said below
- queries: bfloat16 [32, 2, 64, 576], P(('groups', 'seq'), None, 'head'), parts along dimension 0, may hold values from -82 to 82
- new_hidden: bfloat16 [32, 2, 7168], P(('groups', 'seq'), None, 'head'), parts along dimension 0, may hold values from -6 to 6
- kv_down: bfloat16 [7168, 576], P('head'), may hold values from -0.0625 to 0.0625
- kv_gain: float32 [512], replicated, may hold values from 0.1 to 1.9
- value_up: bfloat16 [64, 512, 128], P('head'), may hold values from -0.5 to 0.5
Outputs:
- new_rows: bfloat16 [32, 2, 576], P(('groups', 'seq')), parts along dimension 0
- attended: bfloat16 [32, 2, 64, 128], P(('groups', 'seq'), None, 'head'), parts along dimension 0
The draws below stay inside these ranges and needn't reach their ends.
There are 2 independent parts, one for each index of `groups`. The reference program is written for one: setup_inputs(seed, part) draws one part's arguments, and reference() takes and returns one part's arrays. A program takes and returns all parts, laid end to end along the dimension named above; an argument that names none is the same for every part. Nothing has to cross between parts.
Inputs may be any that keep to these rules, and one draw needn't show every extreme that they name: `page_table`: row p lists the pool pages of prompt p in order, entry j holding its positions j * 128 to j * 128 + 127; after its first ceil(prompt_len[p] / 128) entries it is -1; no pool page is listed twice. Pool page q is row q % 48 of the seq device q // 48. `prompt_len`: one prompt has exactly 16384 tokens, every other one at most 16384. `host_samples`: each sample appears once. Sample s is fork s % 8 of prompt s // 8; slot i is served by the seq device i // 2. `cache_pool`: pool pages that no prompt lists hold arbitrary values.
All inputs are finite; a program needn't handle non-finite values.
Results may differ from the reference program's by a relative error of at most 0.003.
Values may be sent and summed in bfloat16 or wider, within the bound.
A program may use at most 128 MiB of HBM per device.

```python
import jax
import jax.numpy as jnp
from jax import lax

D = 7168
LAT = 512
ROPE = 64
VHEAD = 128
HEADS = 64
FORK = 8
PAGE = 128
SAMPLES = 16
PROMPTS = 2
POOL = 384
LONGEST = 16384
SHORTEST = 2048
CAPLEN = 16384
MAXPAGES = 128


def layout(key):
    key = jax.random.fold_in(key, 7)
    key_len, key_long, key_perm, key_host = jax.random.split(key, 4)
    others = jax.random.randint(key_len, (PROMPTS,), SHORTEST, CAPLEN + 1)
    longest_at = jax.random.randint(key_long, (), 0, PROMPTS)
    lengths = jnp.where(jnp.arange(PROMPTS) == longest_at, LONGEST, others).astype(jnp.int32)
    counts = (lengths + PAGE - 1) // PAGE
    starts = jnp.cumsum(counts) - counts
    shuffled = jax.random.permutation(key_perm, POOL).astype(jnp.int32)
    front_page = shuffled[0]
    shuffled = jnp.where(shuffled == POOL - 1, front_page, shuffled).at[0].set(POOL - 1)
    column = jnp.arange(MAXPAGES, dtype=jnp.int32)
    position = jnp.minimum(starts[:, None] + column[None, :], POOL - 1)
    page_ids = jnp.where(column[None, :] < counts[:, None], shuffled[position], -1).astype(jnp.int32)
    host_ids = jax.random.permutation(key_host, SAMPLES).astype(jnp.int32)
    return (lengths, page_ids, host_ids)


def draw_prompt_len(key, part):
    lengths, page_ids, host_ids = layout(key)
    return lengths


def draw_page_table(key, part):
    lengths, page_ids, host_ids = layout(key)
    return page_ids


def draw_host_samples(key, part):
    lengths, page_ids, host_ids = layout(key)
    return host_ids


def draw_cache_pool(key, part):
    key = jax.random.fold_in(key, 3)
    full_shape = (POOL, PAGE, LAT + ROPE)
    pool_rows = jnp.clip(jax.random.normal(key, full_shape, jnp.float32), -6.0, 6.0)
    return pool_rows.astype(jnp.bfloat16)


def draw_queries(key, part):
    key = jax.random.fold_in(key, 5)
    key_base = jax.random.fold_in(key, 0)
    full_shape = (SAMPLES, 2, HEADS, LAT + ROPE)
    drawn = jnp.clip(2.5 * jax.random.normal(key_base, full_shape, jnp.float32), -15.0, 15.0)
    return drawn.astype(jnp.bfloat16)


def block_levels(own_key, dims, shards, smallest, largest):
    loudness = 1.0
    for dim, blocks in shards:
        heights = jax.random.uniform(jax.random.fold_in(jax.random.fold_in(own_key, 6), dim), (blocks,), jnp.float32, smallest / len(shards), largest / len(shards))
        loudness = loudness * jnp.repeat(jnp.exp(heights), dims[dim] // blocks).reshape((-1,) + (1,) * (len(dims) - 1 - dim))
    return loudness


def bell_draw(rng, shape, width, reach, pieces=(), kind=jnp.bfloat16):
    result = width * jax.random.normal(rng, shape, jnp.float32)
    if pieces:
        result = result * block_levels(rng, shape, pieces, -0.22, 0.18)
    return jnp.clip(result, -reach, reach).astype(kind)


def setup_inputs(seed: int = 0, part: int = 0) -> dict:
    key_of = jax.random.split(jax.random.key(seed), 10)
    part_splits = jax.random.split(jax.random.fold_in(key_of[9], part), 10)
    return {
        "cache_pool": draw_cache_pool(jax.random.fold_in(jax.random.fold_in(key_of[9], part), 71), part),
        "page_table": draw_page_table(jax.random.fold_in(jax.random.fold_in(key_of[9], part), 71), part),
        "prompt_len": draw_prompt_len(jax.random.fold_in(jax.random.fold_in(key_of[9], part), 71), part),
        "host_samples": draw_host_samples(jax.random.fold_in(jax.random.fold_in(key_of[9], part), 71), part),
        "queries": draw_queries(jax.random.fold_in(jax.random.fold_in(key_of[9], part), 71), part),
        "new_hidden": bell_draw(part_splits[5], (SAMPLES, 2, D), 1.0, 6.0, ((0, 8), (2, 2))),
        "kv_down": bell_draw(key_of[6], (D, LAT + ROPE), D ** -0.5, 0.0625, ((0, 2),)),
        "kv_gain": jnp.clip(1.0 + 0.18 * jax.random.normal(key_of[7], (LAT,), jnp.float32), 0.1, 1.9),
        "value_up": bell_draw(key_of[8], (HEADS, LAT, VHEAD), (LAT // 4) ** -0.5, 0.5, ((0, 2),)),
    }


eps = 1e-06
score_scale = 192.0 ** (-0.5)
floor_score = -1e+30

def finish_rows(raw_rows, row_gain):
    latent_width = row_gain.shape[0]
    latent = raw_rows[..., :latent_width]
    spread = lax.rsqrt(lax.optimization_barrier(jnp.mean(latent * latent, axis=-1, keepdims=True)) + eps)
    normed = latent * spread * row_gain
    return jnp.concatenate([normed, raw_rows[..., latent_width:]], axis=-1).astype(jnp.bfloat16)

def reference(cache_pool, page_table, prompt_len, host_samples, queries, new_hidden, kv_down, kv_gain, value_up):
    new_rows = finish_rows(jnp.dot(new_hidden, kv_down, preferred_element_type=jnp.float32), kv_gain)
    row_count = FORK * 2 * HEADS
    sample_ids = jnp.arange(SAMPLES, dtype=jnp.int32)
    slot_index = jnp.zeros((SAMPLES,), jnp.int32).at[host_samples].set(sample_ids)
    query_sample = queries[slot_index].astype(jnp.float32)
    fresh_sample = new_rows[slot_index].astype(jnp.float32)
    query_prompt = query_sample.reshape(PROMPTS, row_count, LAT + ROPE)
    flat_table = page_table.reshape(-1)
    target = jnp.where(flat_table >= 0, flat_table, POOL).astype(jnp.int32)
    owner_prompt = jnp.repeat(jnp.arange(PROMPTS, dtype=jnp.int32), MAXPAGES)
    owner_number = jnp.tile(jnp.arange(MAXPAGES, dtype=jnp.int32), PROMPTS)
    page_prompt = jnp.zeros((POOL,), jnp.int32).at[target].set(owner_prompt, mode='drop')
    page_number = jnp.zeros((POOL,), jnp.int32).at[target].set(owner_number, mode='drop')
    page_live = jnp.zeros((POOL,), jnp.int32).at[target].set(jnp.ones_like(owner_prompt), mode='drop')
    live_rows = jnp.where(page_live > 0, prompt_len[page_prompt] - page_number * PAGE, 0).astype(jnp.int32)

    def scores_of(page_keys, prompt_pick, live_count):
        query_block = lax.dynamic_index_in_dim(query_prompt, prompt_pick, 0, keepdims=False)
        scores = jnp.dot(query_block, page_keys.astype(jnp.float32).T, preferred_element_type=jnp.float32) * score_scale
        inside = jnp.arange(PAGE, dtype=jnp.int32) < live_count
        return jnp.where(inside[None, :], scores, floor_score)

    def page_maxima(prompt_top, inputs):
        page_keys, prompt_pick, live_count = inputs
        row_best = lax.optimization_barrier(jnp.max(scores_of(page_keys, prompt_pick, live_count), axis=1))
        current = lax.dynamic_index_in_dim(prompt_top, prompt_pick, 0, keepdims=True)
        updated = jnp.maximum(current, row_best[None])
        return (lax.dynamic_update_index_in_dim(prompt_top, updated, prompt_pick, 0), None)
    start_top = jnp.full((PROMPTS, row_count), floor_score, jnp.float32)
    prompt_top, _ = lax.scan(page_maxima, start_top, (cache_pool, page_prompt, live_rows))
    fresh_scores = jnp.einsum('sthk,sjk->sthj', query_sample, fresh_sample) * score_scale
    steps_seen = jnp.arange(2)[None, None, None, :] <= jnp.arange(2)[None, :, None, None]
    fresh_scores = jnp.where(steps_seen, fresh_scores, floor_score)
    row_max = jnp.maximum(prompt_top.reshape(SAMPLES, 2, HEADS), lax.optimization_barrier(jnp.max(fresh_scores, axis=3)))
    prompt_max = row_max.reshape(PROMPTS, row_count)

    def page_totals(carry, inputs):
        latent_sums, weight_total = carry
        page_keys, prompt_pick, live_count = inputs
        scores = scores_of(page_keys, prompt_pick, live_count)
        row_best = lax.dynamic_index_in_dim(prompt_max, prompt_pick, 0, keepdims=False)
        weights = jnp.exp(scores - row_best[:, None])
        rounded = lax.optimization_barrier(weights.astype(jnp.bfloat16)).astype(jnp.float32)
        page_part = jnp.dot(rounded, page_keys[:, :LAT].astype(jnp.float32), preferred_element_type=jnp.float32)
        current = lax.dynamic_index_in_dim(latent_sums, prompt_pick, 0, keepdims=True)
        latent_sums = lax.dynamic_update_index_in_dim(latent_sums, current + page_part[None], prompt_pick, 0)
        current_total = lax.dynamic_index_in_dim(weight_total, prompt_pick, 0, keepdims=True)
        weight_total = lax.dynamic_update_index_in_dim(weight_total, current_total + lax.optimization_barrier(jnp.sum(weights, axis=1))[None], prompt_pick, 0)
        return ((latent_sums, weight_total), None)
    empty_sums = (jnp.zeros((PROMPTS, row_count, LAT), jnp.float32), jnp.zeros((PROMPTS, row_count), jnp.float32))
    (latent_sums, weight_total), _ = lax.scan(page_totals, empty_sums, (cache_pool, page_prompt, live_rows))
    fresh_weights = jnp.exp(fresh_scores - row_max[..., None])
    fresh_rounded = lax.optimization_barrier(fresh_weights.astype(jnp.bfloat16)).astype(jnp.float32)
    fresh_sums = jnp.einsum('sthj,sjl->sthl', fresh_rounded, fresh_sample[..., :LAT])
    weight_total = weight_total.reshape(SAMPLES, 2, HEADS) + lax.optimization_barrier(jnp.sum(fresh_weights, axis=3))
    latent_out = (latent_sums.reshape(SAMPLES, 2, HEADS, LAT) + fresh_sums) / weight_total[..., None]
    attended = jnp.einsum('sthl,hlv->sthv', latent_out, value_up.astype(jnp.float32), precision=lax.Precision.HIGHEST)
    return (new_rows, attended.astype(jnp.bfloat16)[host_samples])
```

```python
import functools

import jax
import jax.numpy as jnp
from jax import lax
from jax.experimental import pallas as pl
from jax.experimental.pallas import tpu as pltpu
from jax.sharding import PartitionSpec as P

eps = 1e-06
log2_scale = 192.0 ** (-0.5) * 1.4426950408889634
floor_score = -1e30
block_pages = 4
fork_count = 8
mesh_ids = pl.DeviceIdType.MESH
vmem = pl.BlockSpec(memory_space=pltpu.VMEM)
smem = pl.BlockSpec(memory_space=pltpu.SMEM)
anywhere = pl.BlockSpec(memory_space=pl.ANY)
trans_b = (((1,), (1,)), ((), ()))


def gather_kernel(
    n, q_ref, hs_ref, nh_ref, down_ref, gain_ref, qall_ref, hsall_ref, rows_ref,
    down_buf, raw_mine, raw_other, down_sem, own_sem, q_send, q_recv, hs_send, hs_recv,
    raw_send, raw_recv,
):
    minor = 2
    major = n // minor
    me = lax.axis_index("seq")
    a, b = me // minor, me % minor
    head = lax.axis_index("head")
    down_copy = pltpu.make_async_copy(down_ref, down_buf, down_sem)
    down_copy.start()
    barrier = pltpu.get_barrier_semaphore()

    def greet(where):
        pl.semaphore_signal(barrier, inc=1, device_id=where, device_id_type=mesh_ids)

    @pl.when(a > 0)
    def _():
        greet({"seq": me - minor})

    @pl.when(a < major - 1)
    def _():
        greet({"seq": me + minor})

    mate = a * minor + (1 - b)
    greet({"seq": mate})
    greet({"head": 1 - head})
    near = jnp.where(a > 0, 1, 0) + jnp.where(a < major - 1, 1, 0)
    pl.semaphore_wait(barrier, 2 + near)

    def copies(src, first, way, dest):
        return (
            pltpu.make_async_remote_copy(
                src_ref=q_ref if first else qall_ref.at[src],
                dst_ref=qall_ref.at[src],
                send_sem=q_send.at[src, way],
                recv_sem=q_recv.at[src],
                device_id={"seq": dest},
                device_id_type=mesh_ids,
            ),
            pltpu.make_async_remote_copy(
                src_ref=hs_ref if first else hsall_ref.at[src],
                dst_ref=hsall_ref.at[src],
                send_sem=hs_send.at[src, way],
                recv_sem=hs_recv.at[src],
                device_id={"seq": dest},
                device_id_type=mesh_ids,
            ),
        )

    def send(src, first, way, dest):
        for copy in copies(src, first, way, dest):
            copy.start()

    def await_send(src, first, way, dest):
        for copy in copies(src, first, way, dest):
            copy.wait_send()

    def await_recv(src):
        for copy in copies(src, False, 0, me):
            copy.wait_recv()

    @pl.when(a > 0)
    def _():
        send(me, True, 0, me - minor)

    @pl.when(a < major - 1)
    def _():
        send(me, True, 1, me + minor)

    send(me, True, 2, mate)
    own_q = pltpu.make_async_copy(q_ref, qall_ref.at[me], own_sem.at[0])
    own_hs = pltpu.make_async_copy(hs_ref, hsall_ref.at[me], own_sem.at[1])
    own_q.start()
    own_hs.start()
    down_copy.wait()
    raw_mine[...] = lax.dot_general(
        nh_ref[...], down_buf[...], trans_b, preferred_element_type=jnp.float32
    )[0:8]
    raw_copy = pltpu.make_async_remote_copy(
        src_ref=raw_mine,
        dst_ref=raw_other,
        send_sem=raw_send,
        recv_sem=raw_recv,
        device_id={"head": 1 - head},
        device_id_type=mesh_ids,
    )
    raw_copy.start()

    def forward_down(d):
        src = me + d * minor

        @pl.when(a + d < major)
        def _():
            await_recv(src)

            @pl.when(a > 0)
            def _():
                send(src, False, 0, me - minor)

            send(src, False, 2, mate)

    def forward_up(d):
        src = me - d * minor

        @pl.when(a - d >= 0)
        def _():
            await_recv(src)

            @pl.when(a < major - 1)
            def _():
                send(src, False, 1, me + minor)

            send(src, False, 2, mate)

    for d in range(1, major):
        forward_down(d)
        forward_up(d)
        if d == 1:
            raw_copy.wait()
            raw = raw_mine[...] + raw_other[...]
            width = gain_ref.shape[1]
            latent = raw[:, :width]
            spread = lax.rsqrt(jnp.mean(latent * latent, axis=-1, keepdims=True) + eps)
            rows_ref[0:8, :width] = (latent * spread * gain_ref[...]).astype(jnp.bfloat16)
            rows_ref[0:8, width:] = raw[:, width:].astype(jnp.bfloat16)
            rows_ref[8:16, :] = jnp.zeros((8, raw.shape[1]), jnp.bfloat16)
    for c in range(major):
        await_recv(c * minor + (1 - b))
    own_q.wait()
    own_hs.wait()

    for c in range(major):
        src = c * minor + b

        @pl.when(jnp.logical_and(a > 0, c >= a))
        def _():
            await_send(src, False, 0, me - minor)

        @pl.when(jnp.logical_and(a < major - 1, c <= a))
        def _():
            await_send(src, False, 1, me + minor)

        await_send(src, False, 2, mate)


def attend_kernel(
    list_ref, live_ref, count_ref, hs_ref, q_ref, fresh_ref, pool_ref, up_ref, o_ref, ml_ref,
    kbuf, sbuf, sfresh, qp, acc, oacc, mbuf, lbuf, mlcol, upbuf, slot_of, page_sem, up_sem,
):
    prompts = list_ref.shape[0]
    per_host = 2
    slots, slot_rows, width = q_ref.shape
    heads, latent, vhead = up_ref.shape
    rows = fork_count * slot_rows
    me = lax.axis_index("seq")

    def page_copy(p, i, at):
        return pltpu.make_async_copy(pool_ref.at[list_ref[p, i]], kbuf.at[at], page_sem.at[at])

    def blocks_of(p):
        return (count_ref[p] + block_pages - 1) // block_pages

    def start_prompt(p, base):
        count = blocks_of(p) * block_pages

        def start_page(i, carry):
            page_copy(p, i, base + i).start()
            return carry

        lax.fori_loop(0, count, start_page, 0)
        return base + count

    lax.fori_loop(0, prompts, start_prompt, 0)
    up_copy = pltpu.make_async_copy(up_ref, upbuf, up_sem)
    up_copy.start()

    def note_slot(i, carry):
        slot_of[hs_ref[i // per_host, 0, i % per_host]] = i
        return carry

    lax.fori_loop(0, slots, note_slot, 0)
    lane = lax.broadcasted_iota(jnp.int32, (1, 128), 1)
    fresh_lane = lax.broadcasted_iota(jnp.int32, (slot_rows, 16), 1)
    step_of = lax.broadcasted_iota(jnp.int32, (slot_rows, 16), 0) // heads
    step_ok = jnp.logical_and(fresh_lane % 2 <= step_of, fresh_lane < 2 * per_host)

    def one_prompt(p, base):
        for f in range(fork_count):
            qp[f * slot_rows : (f + 1) * slot_rows, :] = q_ref[slot_of[p * fork_count + f]]
        fresh_all = (
            lax.dot_general(qp[...], fresh_ref[...], trans_b, preferred_element_type=jnp.float32)
            * log2_scale
        )
        for f in range(fork_count):
            part = slice(f * slot_rows, (f + 1) * slot_rows)
            mine = slot_of[p * fork_count + f] - me * per_host
            seen = jnp.logical_and(step_ok, fresh_lane // 2 == mine)
            scores = jnp.where(seen, fresh_all[part], floor_score)
            sfresh[part, :] = scores
            mbuf[part, :] = jnp.broadcast_to(
                jnp.max(scores, axis=1, keepdims=True), (slot_rows, 128)
            )
        blocks = blocks_of(p)

        def score_block(j, carry):
            for i in range(block_pages):
                page_copy(p, j * block_pages + i, base + j * block_pages + i).wait()
            keys = jnp.concatenate(
                [kbuf[base + j * block_pages + i] for i in range(block_pages)], axis=1
            )
            scores = jnp.dot(qp[...], keys, preferred_element_type=jnp.float32) * log2_scale
            top = mbuf[...]
            for i in range(block_pages):
                live = live_ref[p, j * block_pages + i]
                piece = jnp.where(lane < live, scores[:, i * 128 : (i + 1) * 128], floor_score)
                sbuf[j, :, i * 128 : (i + 1) * 128] = piece
                top = jnp.maximum(top, piece)
            mbuf[...] = top
            return carry

        lax.fori_loop(0, blocks, score_block, 0)
        top = jnp.max(mbuf[...], axis=1, keepdims=True)
        mbuf[...] = jnp.broadcast_to(top, (rows, 128))
        fresh_scores = sfresh[...]
        fresh_w = jnp.where(fresh_scores > floor_score, jnp.exp2(fresh_scores - top), 0.0)
        fresh_total = jnp.sum(fresh_w, axis=1, keepdims=True)
        lbuf[...] = jnp.where(lane == 0, fresh_total, 0.0)
        fresh_w = fresh_w.astype(jnp.bfloat16)
        for c in range(latent // 128):
            acc[c] = jnp.dot(
                fresh_w, fresh_ref[:, c * 128 : (c + 1) * 128], preferred_element_type=jnp.float32
            )

        def add_block(j, carry):
            keys = jnp.concatenate(
                [kbuf[base + j * block_pages + i, :latent] for i in range(block_pages)], axis=1
            )
            top = mbuf[...]
            total = lbuf[...]
            rounded = []
            for i in range(block_pages):
                w = jnp.exp2(sbuf[j, :, i * 128 : (i + 1) * 128] - top)
                total = total + w
                rounded.append(w.astype(jnp.bfloat16))
            lbuf[...] = total
            part = lax.dot_general(
                jnp.concatenate(rounded, axis=1), keys, trans_b,
                preferred_element_type=jnp.float32,
            )
            for c in range(latent // 128):
                acc[c] += part[:, c * 128 : (c + 1) * 128]
            return carry

        lax.fori_loop(0, blocks, add_block, 0)
        total = jnp.sum(lbuf[...], axis=1, keepdims=True)
        ml = jnp.where(lane == 0, mbuf[...], total)

        @pl.when(p == 0)
        def _():
            up_copy.wait()

        group = 2 * fork_count
        for h in range(heads):
            x = jnp.concatenate(
                [acc[c, pl.ds(h, group, stride=heads), :] for c in range(latent // 128)], axis=1
            )
            hi = x.astype(jnp.bfloat16)
            lo = (x - hi.astype(jnp.float32)).astype(jnp.bfloat16)
            y = jnp.dot(
                jnp.concatenate([hi, lo], axis=0), upbuf[h], preferred_element_type=jnp.float32
            )
            oacc[pl.ds(h, group, stride=heads), :] = y[:group] + y[group:]
        for f in range(fork_count):
            part = slice(f * slot_rows, (f + 1) * slot_rows)
            slot = slot_of[p * fork_count + f]
            o_ref[slot] = oacc[part, :]
            mlcol[slot] = ml[part]
        return base + blocks * block_pages

    lax.fori_loop(0, prompts, one_prompt, 0)

    def turn(d, carry):
        both = mlcol[pl.ds(d * per_host, per_host)].reshape(per_host * slot_rows, 128)
        ml_ref[d] = both.T[0:8]
        return carry

    lax.fori_loop(0, slots // per_host, turn, 0)


def combine_kernel(
    n, o_ref, ml_ref, out_ref, o_got, ml_got, gains, o_send, o_recv, ml_send, ml_recv
):
    me = lax.axis_index("seq")
    barrier = pltpu.get_barrier_semaphore()
    for k in range(1, n):
        pl.semaphore_signal(
            barrier, inc=1, device_id={"seq": (me + k) % n}, device_id_type=mesh_ids
        )
    pl.semaphore_wait(barrier, n - 1)
    copies = []
    for k in range(1, n):
        dest = (me + k) % n
        for src, got, s_sem, r_sem in (
            (ml_ref, ml_got, ml_send, ml_recv),
            (o_ref, o_got, o_send, o_recv),
        ):
            copy = pltpu.make_async_remote_copy(
                src_ref=src.at[dest],
                dst_ref=got.at[k],
                send_sem=s_sem.at[k],
                recv_sem=r_sem.at[k],
                device_id={"seq": dest},
                device_id_type=mesh_ids,
            )
            copy.start()
            copies.append(copy)
    ml_got[0] = ml_ref[me]
    o_got[0] = o_ref[me]
    for copy in copies:
        copy.wait()
    top = ml_got[0, 0:1, :]
    for k in range(1, n):
        top = jnp.maximum(top, ml_got[k, 0:1, :])
    total = jnp.zeros_like(top)
    gains[...] = jnp.zeros_like(gains)
    for k in range(n):
        factor = jnp.exp2(ml_got[k, 0:1, :] - top)
        gains[k : k + 1, :] = factor
        total = total + factor * ml_got[k, 1:2, :]
    turned = (gains[...] / total).T
    out = turned[:, 0:1] * o_got[0]
    for k in range(1, n):
        out = out + turned[:, k : k + 1] * o_got[k]
    out_ref[...] = out.astype(jnp.bfloat16)


def on_device(
    cache_pool, page_table, prompt_len, host_samples, queries, new_hidden, kv_down, kv_gain,
    value_up,
):
    n = lax.axis_size("seq")
    me = lax.axis_index("seq")
    per_host, steps, heads, width = queries.shape
    latent = kv_gain.shape[0]
    vhead = value_up.shape[2]
    page_count, page_rows = cache_pool.shape[:2]
    prompts, table_width = page_table.shape
    host_rows = per_host * steps * heads
    slot_rows = steps * heads
    slots = n * per_host
    rows = fork_count * slot_rows
    local = page_table - me * page_count
    owned = jnp.logical_and(local >= 0, local < page_count)
    column = jnp.arange(table_width, dtype=jnp.int32)
    before = column[None, :] < column[:, None]
    rank = jnp.sum(
        jnp.where(jnp.logical_and(before[None], owned[:, None, :]), 1, 0), axis=2, dtype=jnp.int32
    )
    list_width = -(-page_count // block_pages) * block_pages
    order = jnp.arange(list_width, dtype=jnp.int32)
    hot = jnp.logical_and(owned[:, None, :], rank[:, None, :] == order[None, :, None])
    page_list = jnp.sum(jnp.where(hot, local[:, None, :], 0), axis=2, dtype=jnp.int32)
    left = jnp.minimum(prompt_len[:, None] - column[None, :] * page_rows, page_rows)
    page_live = jnp.sum(jnp.where(hot, left[:, None, :], 0), axis=2, dtype=jnp.int32)
    counts = jnp.sum(owned, axis=1, dtype=jnp.int32)

    hs_tile = jnp.pad(host_samples[None, :], ((0, 7), (0, 128 - per_host)))
    hidden = jnp.pad(
        new_hidden.reshape(per_host * steps, -1), ((0, 16 - per_host * steps), (0, 0))
    )
    big = pltpu.CompilerParams
    qall, hsall, rows16 = pl.pallas_call(
        functools.partial(gather_kernel, n),
        out_shape=(
            jax.ShapeDtypeStruct((n, host_rows, width), jnp.bfloat16),
            jax.ShapeDtypeStruct((n, 8, 128), jnp.int32),
            jax.ShapeDtypeStruct((16, width), jnp.bfloat16),
        ),
        in_specs=[vmem, vmem, vmem, anywhere, vmem],
        out_specs=(vmem, vmem, vmem),
        scratch_shapes=[
            pltpu.VMEM(kv_down.shape[::-1], jnp.bfloat16),
            pltpu.VMEM((8, width), jnp.float32),
            pltpu.VMEM((8, width), jnp.float32),
            pltpu.SemaphoreType.DMA,
            pltpu.SemaphoreType.DMA((2,)),
            pltpu.SemaphoreType.DMA((n, 3)),
            pltpu.SemaphoreType.DMA((n,)),
            pltpu.SemaphoreType.DMA((n, 3)),
            pltpu.SemaphoreType.DMA((n,)),
            pltpu.SemaphoreType.DMA,
            pltpu.SemaphoreType.DMA,
        ],
        compiler_params=big(
            collective_id=0, has_side_effects=True, vmem_limit_bytes=48 * 2**20
        ),
    )(queries.reshape(host_rows, width), hs_tile, hidden, kv_down.T, kv_gain[None, :])
    new_rows = rows16[: per_host * steps].reshape(per_host, steps, width)

    slots_held = -(-page_count // block_pages) * block_pages + (block_pages - 1) * prompts
    o, ml = pl.pallas_call(
        attend_kernel,
        out_shape=(
            jax.ShapeDtypeStruct((slots, slot_rows, vhead), jnp.float32),
            jax.ShapeDtypeStruct((n, 8, 128), jnp.float32),
        ),
        in_specs=[smem, smem, smem, smem, vmem, vmem, anywhere, anywhere],
        out_specs=(vmem, vmem),
        scratch_shapes=[
            pltpu.VMEM((slots_held, width, page_rows), jnp.bfloat16),
            pltpu.VMEM((list_width // block_pages, rows, block_pages * page_rows), jnp.float32),
            pltpu.VMEM((rows, 16), jnp.float32),
            pltpu.VMEM((rows, width), jnp.bfloat16),
            pltpu.VMEM((latent // 128, rows, 128), jnp.float32),
            pltpu.VMEM((rows, vhead), jnp.float32),
            pltpu.VMEM((rows, 128), jnp.float32),
            pltpu.VMEM((rows, 128), jnp.float32),
            pltpu.VMEM((slots, slot_rows, 128), jnp.float32),
            pltpu.VMEM(value_up.shape, jnp.bfloat16),
            pltpu.SMEM((slots,), jnp.int32),
            pltpu.SemaphoreType.DMA((slots_held,)),
            pltpu.SemaphoreType.DMA,
        ],
        compiler_params=big(vmem_limit_bytes=60 * 2**20),
    )(
        page_list, page_live, counts, hsall, qall.reshape(slots, slot_rows, width), rows16,
        jnp.swapaxes(cache_pool, 1, 2), value_up,
    )

    out = pl.pallas_call(
        functools.partial(combine_kernel, n),
        out_shape=jax.ShapeDtypeStruct((host_rows, vhead), jnp.bfloat16),
        in_specs=[vmem, vmem],
        out_specs=vmem,
        scratch_shapes=[
            pltpu.VMEM((n, host_rows, vhead), jnp.float32),
            pltpu.VMEM((n, 8, 128), jnp.float32),
            pltpu.VMEM((128, 128), jnp.float32),
            pltpu.SemaphoreType.DMA((n,)),
            pltpu.SemaphoreType.DMA((n,)),
            pltpu.SemaphoreType.DMA((n,)),
            pltpu.SemaphoreType.DMA((n,)),
        ],
        compiler_params=big(
            collective_id=1, has_side_effects=True, vmem_limit_bytes=48 * 2**20
        ),
    )(o.reshape(n, host_rows, vhead), ml)
    return (new_rows, out.reshape(per_host, steps, heads, vhead))


def solution(mesh):
    in_specs = (
        P(("groups", "seq"), None, None),
        P("groups", None),
        P("groups"),
        P(("groups", "seq")),
        P(("groups", "seq"), None, "head", None),
        P(("groups", "seq"), None, "head"),
        P("head", None),
        P(),
        P("head", None, None),
    )
    out_specs = (P(("groups", "seq"), None, None), P(("groups", "seq"), None, "head", None))
    return jax.shard_map(
        on_device, mesh=mesh, in_specs=in_specs, out_specs=out_specs, check_vma=False
    )
```

```python
import functools

import jax
import jax.numpy as jnp
from jax import lax
from jax.experimental import pallas as pl
from jax.experimental.pallas import tpu as pltpu
from jax.sharding import PartitionSpec as P

eps = 1e-06
log2_scale = 192.0 ** (-0.5) * 1.4426950408889634
floor_score = -1e30
block_pages = 4
fork_count = 8
mesh_ids = pl.DeviceIdType.MESH
vmem = pl.BlockSpec(memory_space=pltpu.VMEM)
smem = pl.BlockSpec(memory_space=pltpu.SMEM)
hbm = pl.BlockSpec(memory_space=pltpu.HBM)
trans_b = (((1,), (1,)), ((), ()))


def gather_kernel(
    n, page_count, page_rows, q_ref, host_ref, nh_ref, down_ref, gain_ref, table_ref, len_ref,
    qall_ref, hsall_ref, rows_ref, new_ref, list_ref,
    down_buf, raw_mine, raw_other, nh_buf, hs_ref, rows_buf, list_buf, down_sem, own_sem, q_send,
    q_recv, hs_send, hs_recv, raw_send, raw_recv,
):
    minor = 2
    major = n // minor
    me = lax.axis_index("seq")
    a, b = me // minor, me % minor
    head = lax.axis_index("head")
    half = q_ref.shape[0] // 2
    down_copy = pltpu.make_async_copy(down_ref, down_buf, down_sem)
    down_copy.start()
    barrier = pltpu.get_barrier_semaphore()

    def greet(where):
        pl.semaphore_signal(barrier, inc=1, device_id=where, device_id_type=mesh_ids)

    @pl.when(a > 0)
    def _():
        greet({"seq": me - minor})

    @pl.when(a < major - 1)
    def _():
        greet({"seq": me + minor})

    mate = a * minor + (1 - b)
    greet({"seq": mate})
    greet({"head": 1 - head})
    lane = lax.broadcasted_iota(jnp.int32, (8, 128), 1)
    tile = jnp.zeros((8, 128), jnp.int32)
    for i in range(host_ref.shape[0]):
        tile = jnp.where(lane == i, host_ref[i], tile)
    hs_ref[...] = tile
    near = jnp.where(a > 0, 1, 0) + jnp.where(a < major - 1, 1, 0)
    pl.semaphore_wait(barrier, 2 + near)

    def copies(src, c, first, way, dest):
        rows = pl.ds(c * half, half)
        found = [
            pltpu.make_async_remote_copy(
                src_ref=q_ref.at[rows] if first else qall_ref.at[src, rows],
                dst_ref=qall_ref.at[src, rows],
                send_sem=q_send.at[src, way, c],
                recv_sem=q_recv.at[src, c],
                device_id={"seq": dest},
                device_id_type=mesh_ids,
            )
        ]
        if c == 0:
            found.append(
                pltpu.make_async_remote_copy(
                    src_ref=hs_ref if first else hsall_ref.at[src],
                    dst_ref=hsall_ref.at[src],
                    send_sem=hs_send.at[src, way],
                    recv_sem=hs_recv.at[src],
                    device_id={"seq": dest},
                    device_id_type=mesh_ids,
                )
            )
        return found

    def send(src, c, first, way, dest):
        for copy in copies(src, c, first, way, dest):
            copy.start()

    def await_send(src, first, way, dest):
        for c in range(2):
            for copy in copies(src, c, first, way, dest):
                copy.wait_send()

    def await_recv(src, c):
        for copy in copies(src, c, False, 0, me):
            copy.wait_recv()

    for c in range(2):

        @pl.when(a > 0)
        def _():
            send(me, c, True, 0, me - minor)

        @pl.when(a < major - 1)
        def _():
            send(me, c, True, 1, me + minor)

        send(me, c, True, 2, mate)
    own_q = pltpu.make_async_copy(q_ref, qall_ref.at[me], own_sem.at[0])
    own_hs = pltpu.make_async_copy(hs_ref, hsall_ref.at[me], own_sem.at[1])
    own_q.start()
    own_hs.start()
    per_host, steps = nh_ref.shape[:2]
    nh_buf[...] = jnp.zeros_like(nh_buf)
    for i in range(per_host):
        nh_buf[i * steps : (i + 1) * steps, :] = nh_ref[i].astype(jnp.float32)
    down_copy.wait()
    raw_mine[...] = lax.dot_general(
        nh_buf[...].astype(jnp.bfloat16), down_buf[...], trans_b,
        preferred_element_type=jnp.float32,
    )
    raw_copy = pltpu.make_async_remote_copy(
        src_ref=raw_mine,
        dst_ref=raw_other,
        send_sem=raw_send,
        recv_sem=raw_recv,
        device_id={"head": 1 - head},
        device_id_type=mesh_ids,
    )
    raw_copy.start()

    def forward_down(d, c):
        src = me + d * minor

        @pl.when(a + d < major)
        def _():
            await_recv(src, c)

            @pl.when(a > 0)
            def _():
                send(src, c, False, 0, me - minor)

            send(src, c, False, 2, mate)

    def forward_up(d, c):
        src = me - d * minor

        @pl.when(a - d >= 0)
        def _():
            await_recv(src, c)

            @pl.when(a < major - 1)
            def _():
                send(src, c, False, 1, me + minor)

            send(src, c, False, 2, mate)

    def page_lists():
        prompts, table_width = table_ref.shape
        list_width = list_buf.shape[2]
        column = lax.broadcasted_iota(jnp.int32, (1, table_width), 1)
        earlier = lax.broadcasted_iota(jnp.int32, (table_width, table_width), 0)
        later = lax.broadcasted_iota(jnp.int32, (table_width, table_width), 1)
        before = jnp.where(earlier < later, 1.0, 0.0).astype(jnp.bfloat16)
        order = lax.broadcasted_iota(jnp.int32, (list_width, table_width), 0)
        line = lax.broadcasted_iota(jnp.int32, (8, table_width), 0)
        for p in range(prompts):
            local = table_ref[p : p + 1, :] - me * page_count
            owned = jnp.where(jnp.logical_and(local >= 0, local < page_count), 1, 0)
            many = jnp.broadcast_to(owned, (8, table_width)).astype(jnp.float32)
            rank = jnp.dot(
                many.astype(jnp.bfloat16), before, preferred_element_type=jnp.float32
            )[0:1].astype(jnp.int32)
            hot = jnp.where(jnp.logical_and(order == rank, owned > 0), 1.0, 0.0)
            left = jnp.minimum(len_ref[p] - column * page_rows, page_rows)
            count = jnp.sum(owned, axis=1, keepdims=True)
            values = jnp.where(line == 0, local * owned, left * owned).astype(jnp.float32)
            picked = lax.dot_general(
                values.astype(jnp.bfloat16), hot.astype(jnp.bfloat16), trans_b,
                preferred_element_type=jnp.float32,
            ).astype(jnp.int32)
            picked_line = lax.broadcasted_iota(jnp.int32, picked.shape, 0)
            list_buf[p] = jnp.where(picked_line == 2, count, picked)

    width = gain_ref.shape[1]
    extra = []
    for d in range(1, major):
        for c in range(2):
            forward_down(d, c)
            forward_up(d, c)
        if d == 1:
            raw_copy.wait()
            raw = raw_mine[...] + raw_other[...]
            latent = raw[:, :width]
            spread = lax.rsqrt(jnp.mean(latent * latent, axis=-1, keepdims=True) + eps)
            done = jnp.concatenate(
                [latent * spread * gain_ref[...], raw[:, width:]], axis=1
            )
            rows_buf[...] = jnp.concatenate([done, jnp.zeros_like(done)], axis=0).astype(
                jnp.bfloat16
            )
            for i in range(per_host):
                new_ref[i] = done[i * steps : (i + 1) * steps].astype(jnp.bfloat16)
            page_lists()
            extra = [
                pltpu.make_async_copy(rows_buf, rows_ref, own_sem.at[2]),
                pltpu.make_async_copy(list_buf, list_ref, own_sem.at[3]),
            ]
            for copy in extra:
                copy.start()
    for k in range(major):
        for c in range(2):
            await_recv(k * minor + (1 - b), c)
    own_q.wait()
    own_hs.wait()
    for copy in extra:
        copy.wait()
    for k in range(major):
        src = k * minor + b

        @pl.when(jnp.logical_and(a > 0, k >= a))
        def _():
            await_send(src, False, 0, me - minor)

        @pl.when(jnp.logical_and(a < major - 1, k <= a))
        def _():
            await_send(src, False, 1, me + minor)

        await_send(src, False, 2, mate)


def attend_kernel(
    list_ref, hs_ref, q_ref, fresh_ref, pool_ref, up_ref, o_ref, ml_ref,
    kbuf, sbuf, sfresh, qp, acc, oacc, mbuf, lbuf, mlcol, upbuf, slot_of, page_sem, up_sem,
):
    prompts = list_ref.shape[0]
    per_host = 2
    slots, slot_rows, width = q_ref.shape
    heads, latent, vhead = up_ref.shape
    rows = fork_count * slot_rows
    me = lax.axis_index("seq")

    def page_copy(p, i, at):
        return pltpu.make_async_copy(pool_ref.at[list_ref[p, 0, i]], kbuf.at[at], page_sem.at[at])

    def blocks_of(p):
        return (list_ref[p, 2, 0] + block_pages - 1) // block_pages

    def start_prompt(p, base):
        count = blocks_of(p) * block_pages

        def start_page(i, carry):
            page_copy(p, i, base + i).start()
            return carry

        lax.fori_loop(0, count, start_page, 0)
        return base + count

    lax.fori_loop(0, prompts, start_prompt, 0)
    up_copy = pltpu.make_async_copy(up_ref, upbuf, up_sem)
    up_copy.start()

    def note_slot(i, carry):
        slot_of[hs_ref[i // per_host, 0, i % per_host]] = i
        return carry

    lax.fori_loop(0, slots, note_slot, 0)
    lane = lax.broadcasted_iota(jnp.int32, (1, 128), 1)
    fresh_lane = lax.broadcasted_iota(jnp.int32, (slot_rows, 16), 1)
    step_of = lax.broadcasted_iota(jnp.int32, (slot_rows, 16), 0) // heads
    step_ok = jnp.logical_and(fresh_lane % 2 <= step_of, fresh_lane < 2 * per_host)

    def one_prompt(p, base):
        for f in range(fork_count):
            qp[f * slot_rows : (f + 1) * slot_rows, :] = q_ref[slot_of[p * fork_count + f]]
        fresh_all = (
            lax.dot_general(qp[...], fresh_ref[...], trans_b, preferred_element_type=jnp.float32)
            * log2_scale
        )
        for f in range(fork_count):
            part = slice(f * slot_rows, (f + 1) * slot_rows)
            mine = slot_of[p * fork_count + f] - me * per_host
            seen = jnp.logical_and(step_ok, fresh_lane // 2 == mine)
            scores = jnp.where(seen, fresh_all[part], floor_score)
            sfresh[part, :] = scores
            mbuf[part, :] = jnp.broadcast_to(
                jnp.max(scores, axis=1, keepdims=True), (slot_rows, 128)
            )
        blocks = blocks_of(p)

        def score_block(j, carry):
            for i in range(block_pages):
                page_copy(p, j * block_pages + i, base + j * block_pages + i).wait()
            keys = jnp.concatenate(
                [kbuf[base + j * block_pages + i] for i in range(block_pages)], axis=1
            )
            scores = jnp.dot(qp[...], keys, preferred_element_type=jnp.float32) * log2_scale
            top = mbuf[...]
            for i in range(block_pages):
                live = list_ref[p, 1, j * block_pages + i]
                piece = jnp.where(lane < live, scores[:, i * 128 : (i + 1) * 128], floor_score)
                sbuf[j, :, i * 128 : (i + 1) * 128] = piece
                top = jnp.maximum(top, piece)
            mbuf[...] = top
            return carry

        lax.fori_loop(0, blocks, score_block, 0)
        top = jnp.max(mbuf[...], axis=1, keepdims=True)
        mbuf[...] = jnp.broadcast_to(top, (rows, 128))
        fresh_scores = sfresh[...]
        fresh_w = jnp.where(fresh_scores > floor_score, jnp.exp2(fresh_scores - top), 0.0)
        fresh_total = jnp.sum(fresh_w, axis=1, keepdims=True)
        lbuf[...] = jnp.where(lane == 0, fresh_total, 0.0)
        fresh_w = fresh_w.astype(jnp.bfloat16)
        for c in range(latent // 128):
            acc[c] = jnp.dot(
                fresh_w, fresh_ref[:, c * 128 : (c + 1) * 128], preferred_element_type=jnp.float32
            )

        def add_block(j, carry):
            keys = jnp.concatenate(
                [kbuf[base + j * block_pages + i, :latent] for i in range(block_pages)], axis=1
            )
            top = mbuf[...]
            total = lbuf[...]
            rounded = []
            for i in range(block_pages):
                w = jnp.exp2(sbuf[j, :, i * 128 : (i + 1) * 128] - top)
                total = total + w
                rounded.append(w.astype(jnp.bfloat16))
            lbuf[...] = total
            part = lax.dot_general(
                jnp.concatenate(rounded, axis=1), keys, trans_b,
                preferred_element_type=jnp.float32,
            )
            for c in range(latent // 128):
                acc[c] += part[:, c * 128 : (c + 1) * 128]
            return carry

        lax.fori_loop(0, blocks, add_block, 0)
        total = jnp.sum(lbuf[...], axis=1, keepdims=True)
        ml = jnp.where(lane == 0, mbuf[...], total)

        @pl.when(p == 0)
        def _():
            up_copy.wait()

        group = 2 * fork_count
        for h in range(heads):
            x = jnp.concatenate(
                [acc[c, pl.ds(h, group, stride=heads), :] for c in range(latent // 128)], axis=1
            )
            hi = x.astype(jnp.bfloat16)
            lo = (x - hi.astype(jnp.float32)).astype(jnp.bfloat16)
            y = jnp.dot(
                jnp.concatenate([hi, lo], axis=0), upbuf[h], preferred_element_type=jnp.float32
            )
            oacc[pl.ds(h, group, stride=heads), :] = y[:group] + y[group:]
        for f in range(fork_count):
            part = slice(f * slot_rows, (f + 1) * slot_rows)
            slot = slot_of[p * fork_count + f]
            o_ref[slot] = oacc[part, :]
            mlcol[slot] = ml[part]
        return base + blocks * block_pages

    lax.fori_loop(0, prompts, one_prompt, 0)

    def turn(d, carry):
        both = mlcol[pl.ds(d * per_host, per_host)].reshape(per_host * slot_rows, 128)
        ml_ref[d] = both.T[0:8]
        return carry

    lax.fori_loop(0, slots // per_host, turn, 0)


def combine_kernel(
    n, o_ref, ml_ref, out_ref, o_got, ml_got, gains, o_send, o_recv, ml_send, ml_recv
):
    me = lax.axis_index("seq")
    barrier = pltpu.get_barrier_semaphore()
    for k in range(1, n):
        pl.semaphore_signal(
            barrier, inc=1, device_id={"seq": (me + k) % n}, device_id_type=mesh_ids
        )
    pl.semaphore_wait(barrier, n - 1)
    copies = []
    for k in range(1, n):
        dest = (me + k) % n
        for src, got, s_sem, r_sem in (
            (ml_ref, ml_got, ml_send, ml_recv),
            (o_ref, o_got, o_send, o_recv),
        ):
            copy = pltpu.make_async_remote_copy(
                src_ref=src.at[dest],
                dst_ref=got.at[k],
                send_sem=s_sem.at[k],
                recv_sem=r_sem.at[k],
                device_id={"seq": dest},
                device_id_type=mesh_ids,
            )
            copy.start()
            copies.append(copy)
    ml_got[0] = ml_ref[me]
    o_got[0] = o_ref[me]
    for copy in copies:
        copy.wait()
    top = ml_got[0, 0:1, :]
    for k in range(1, n):
        top = jnp.maximum(top, ml_got[k, 0:1, :])
    total = jnp.zeros_like(top)
    gains[...] = jnp.zeros_like(gains)
    for k in range(n):
        factor = jnp.exp2(ml_got[k, 0:1, :] - top)
        gains[k : k + 1, :] = factor
        total = total + factor * ml_got[k, 1:2, :]
    turned = (gains[...] / total).T
    out = turned[:, 0:1] * o_got[0]
    for k in range(1, n):
        out = out + turned[:, k : k + 1] * o_got[k]
    out_ref[...] = out.astype(jnp.bfloat16)


def on_device(
    cache_pool, page_table, prompt_len, host_samples, queries, new_hidden, kv_down, kv_gain,
    value_up,
):
    n = lax.axis_size("seq")
    big = pltpu.CompilerParams
    per_host, steps, heads, width = queries.shape
    latent = kv_gain.shape[0]
    vhead = value_up.shape[2]
    page_count, page_rows = cache_pool.shape[:2]
    prompts = page_table.shape[0]
    host_rows = per_host * steps * heads
    slot_rows = steps * heads
    slots = n * per_host
    rows = fork_count * slot_rows
    list_width = -(-page_count // 128) * 128
    qall, hsall, rows16, new_rows, lists = pl.pallas_call(
        functools.partial(gather_kernel, n, page_count, page_rows),
        out_shape=(
            jax.ShapeDtypeStruct((n, host_rows, width), jnp.bfloat16),
            jax.ShapeDtypeStruct((n, 8, 128), jnp.int32),
            jax.ShapeDtypeStruct((16, width), jnp.bfloat16),
            jax.ShapeDtypeStruct((per_host, steps, width), jnp.bfloat16),
            jax.ShapeDtypeStruct((prompts, 8, list_width), jnp.int32),
        ),
        in_specs=[hbm, smem, vmem, hbm, vmem, vmem, smem],
        out_specs=(hbm, hbm, hbm, vmem, hbm),
        scratch_shapes=[
            pltpu.VMEM(kv_down.shape[::-1], jnp.bfloat16),
            pltpu.VMEM((8, width), jnp.float32),
            pltpu.VMEM((8, width), jnp.float32),
            pltpu.VMEM((8, kv_down.shape[0]), jnp.float32),
            pltpu.VMEM((8, 128), jnp.int32),
            pltpu.VMEM((16, width), jnp.bfloat16),
            pltpu.VMEM((prompts, 8, list_width), jnp.int32),
            pltpu.SemaphoreType.DMA,
            pltpu.SemaphoreType.DMA((4,)),
            pltpu.SemaphoreType.DMA((n, 3, 2)),
            pltpu.SemaphoreType.DMA((n, 2)),
            pltpu.SemaphoreType.DMA((n, 3)),
            pltpu.SemaphoreType.DMA((n,)),
            pltpu.SemaphoreType.DMA,
            pltpu.SemaphoreType.DMA,
        ],
        compiler_params=big(
            collective_id=0, has_side_effects=True, vmem_limit_bytes=20 * 2**20
        ),
    )(
        queries.reshape(host_rows, width), host_samples, new_hidden, kv_down.T, kv_gain[None, :],
        page_table, prompt_len,
    )

    score_blocks = -(-page_count // block_pages)
    slots_held = -(-page_count // block_pages) * block_pages + (block_pages - 1) * prompts
    o, ml = pl.pallas_call(
        attend_kernel,
        out_shape=(
            jax.ShapeDtypeStruct((slots, slot_rows, vhead), jnp.float32),
            jax.ShapeDtypeStruct((n, 8, 128), jnp.float32),
        ),
        in_specs=[smem, smem, vmem, vmem, hbm, hbm],
        out_specs=(vmem, vmem),
        scratch_shapes=[
            pltpu.VMEM((slots_held, width, page_rows), jnp.bfloat16),
            pltpu.VMEM((score_blocks, rows, block_pages * page_rows), jnp.float32),
            pltpu.VMEM((rows, 16), jnp.float32),
            pltpu.VMEM((rows, width), jnp.bfloat16),
            pltpu.VMEM((latent // 128, rows, 128), jnp.float32),
            pltpu.VMEM((rows, vhead), jnp.float32),
            pltpu.VMEM((rows, 128), jnp.float32),
            pltpu.VMEM((rows, 128), jnp.float32),
            pltpu.VMEM((slots, slot_rows, 128), jnp.float32),
            pltpu.VMEM(value_up.shape, jnp.bfloat16),
            pltpu.SMEM((slots,), jnp.int32),
            pltpu.SemaphoreType.DMA((slots_held,)),
            pltpu.SemaphoreType.DMA,
        ],
        compiler_params=big(vmem_limit_bytes=(40 + slots // 8) * 2**20),
    )(
        lists, hsall, qall.reshape(slots, slot_rows, width), rows16,
        jnp.swapaxes(cache_pool, 1, 2), value_up,
    )

    out = pl.pallas_call(
        functools.partial(combine_kernel, n),
        out_shape=jax.ShapeDtypeStruct((host_rows, vhead), jnp.bfloat16),
        in_specs=[vmem, vmem],
        out_specs=vmem,
        scratch_shapes=[
            pltpu.VMEM((n, host_rows, vhead), jnp.float32),
            pltpu.VMEM((n, 8, 128), jnp.float32),
            pltpu.VMEM((128, 128), jnp.float32),
            pltpu.SemaphoreType.DMA((n,)),
            pltpu.SemaphoreType.DMA((n,)),
            pltpu.SemaphoreType.DMA((n,)),
            pltpu.SemaphoreType.DMA((n,)),
        ],
        compiler_params=big(
            collective_id=1, has_side_effects=True, vmem_limit_bytes=16 * 2**20
        ),
    )(o.reshape(n, host_rows, vhead), ml)
    return (new_rows, out.reshape(per_host, steps, heads, vhead))


def solution(mesh):
    in_specs = (
        P(("groups", "seq"), None, None),
        P("groups", None),
        P("groups"),
        P(("groups", "seq")),
        P(("groups", "seq"), None, "head", None),
        P(("groups", "seq"), None, "head"),
        P("head", None),
        P(),
        P("head", None, None),
    )
    out_specs = (P(("groups", "seq"), None, None), P(("groups", "seq"), None, "head", None))
    return jax.shard_map(
        on_device, mesh=mesh, in_specs=in_specs, out_specs=out_specs, check_vma=False
    )
```

```python
import functools

import jax
import jax.numpy as jnp
from jax import lax
from jax.experimental import pallas as pl
from jax.experimental.pallas import tpu as pltpu
from jax.sharding import PartitionSpec as P

eps = 1e-06
log2_scale = 192.0 ** (-0.5) * 1.4426950408889634
floor_score = -1e30
block_pages = 4
fork_count = 8
mesh_ids = pl.DeviceIdType.MESH
vmem = pl.BlockSpec(memory_space=pltpu.VMEM)
smem = pl.BlockSpec(memory_space=pltpu.SMEM)
hbm = pl.BlockSpec(memory_space=pltpu.HBM)
trans_b = (((1,), (1,)), ((), ()))


def gather_kernel(
    n, page_count, page_rows, q_ref, host_ref, nh_hbm, down_ref, gain_hbm, table_hbm, len_ref,
    qall_ref, hsall_ref, rows_ref, new_ref, list_ref,
    down_buf, nh_ref, gain_ref, table_ref, raw_mine, raw_other, nh_buf, hs_ref, rows_buf, new_buf, list_buf, down_sem, own_sem, q_send,
    q_recv, hs_send, hs_recv, raw_send, raw_recv,
):
    minor = 2
    major = n // minor
    me = lax.axis_index("seq")
    a, b = me // minor, me % minor
    head = lax.axis_index("head")
    half = q_ref.shape[0] // 2
    down_copy = pltpu.make_async_copy(down_ref, down_buf, down_sem)
    small = []
    for i, (source, target) in enumerate(
        ((nh_hbm, nh_ref), (gain_hbm, gain_ref), (table_hbm, table_ref))
    ):
        copy = pltpu.make_async_copy(source, target, own_sem.at[5 + i])
        copy.start()
        small.append(copy)
    down_copy.start()
    barrier = pltpu.get_barrier_semaphore()

    def greet(where):
        pl.semaphore_signal(barrier, inc=1, device_id=where, device_id_type=mesh_ids)

    @pl.when(a > 0)
    def _():
        greet({"seq": me - minor})

    @pl.when(a < major - 1)
    def _():
        greet({"seq": me + minor})

    mate = a * minor + (1 - b)
    greet({"seq": mate})
    greet({"head": 1 - head})
    lane = lax.broadcasted_iota(jnp.int32, (8, 128), 1)
    tile = jnp.zeros((8, 128), jnp.int32)
    for i in range(host_ref.shape[0]):
        tile = jnp.where(lane == i, host_ref[i], tile)
    hs_ref[...] = tile
    near = jnp.where(a > 0, 1, 0) + jnp.where(a < major - 1, 1, 0)
    pl.semaphore_wait(barrier, 2 + near)

    def copies(src, c, first, way, dest):
        rows = pl.ds(c * half, half)
        found = [
            pltpu.make_async_remote_copy(
                src_ref=q_ref.at[rows] if first else qall_ref.at[src, rows],
                dst_ref=qall_ref.at[src, rows],
                send_sem=q_send.at[src, way, c],
                recv_sem=q_recv.at[src, c],
                device_id={"seq": dest},
                device_id_type=mesh_ids,
            )
        ]
        if c == 0:
            found.append(
                pltpu.make_async_remote_copy(
                    src_ref=hs_ref if first else hsall_ref.at[src],
                    dst_ref=hsall_ref.at[src],
                    send_sem=hs_send.at[src, way],
                    recv_sem=hs_recv.at[src],
                    device_id={"seq": dest},
                    device_id_type=mesh_ids,
                )
            )
        return found

    def send(src, c, first, way, dest):
        for copy in copies(src, c, first, way, dest):
            copy.start()

    def await_send(src, first, way, dest):
        for c in range(2):
            for copy in copies(src, c, first, way, dest):
                copy.wait_send()

    def await_recv(src, c):
        for copy in copies(src, c, False, 0, me):
            copy.wait_recv()

    for c in range(2):

        @pl.when(a > 0)
        def _():
            send(me, c, True, 0, me - minor)

        @pl.when(a < major - 1)
        def _():
            send(me, c, True, 1, me + minor)

        send(me, c, True, 2, mate)
    own_q = pltpu.make_async_copy(q_ref, qall_ref.at[me], own_sem.at[0])
    own_hs = pltpu.make_async_copy(hs_ref, hsall_ref.at[me], own_sem.at[1])
    own_q.start()
    own_hs.start()
    per_host, steps = nh_ref.shape[:2]
    for copy in small:
        copy.wait()
    nh_buf[...] = jnp.zeros_like(nh_buf)
    for i in range(per_host):
        nh_buf[i * steps : (i + 1) * steps, :] = nh_ref[i].astype(jnp.float32)
    down_copy.wait()
    raw_mine[...] = lax.dot_general(
        nh_buf[...].astype(jnp.bfloat16), down_buf[...], trans_b,
        preferred_element_type=jnp.float32,
    )
    raw_copy = pltpu.make_async_remote_copy(
        src_ref=raw_mine,
        dst_ref=raw_other,
        send_sem=raw_send,
        recv_sem=raw_recv,
        device_id={"head": 1 - head},
        device_id_type=mesh_ids,
    )
    raw_copy.start()

    def forward_down(d, c):
        src = me + d * minor

        @pl.when(a + d < major)
        def _():
            await_recv(src, c)

            @pl.when(a > 0)
            def _():
                send(src, c, False, 0, me - minor)

            send(src, c, False, 2, mate)

    def forward_up(d, c):
        src = me - d * minor

        @pl.when(a - d >= 0)
        def _():
            await_recv(src, c)

            @pl.when(a < major - 1)
            def _():
                send(src, c, False, 1, me + minor)

            send(src, c, False, 2, mate)

    def page_lists():
        prompts, table_width = table_ref.shape
        list_width = list_buf.shape[2]
        column = lax.broadcasted_iota(jnp.int32, (1, table_width), 1)
        earlier = lax.broadcasted_iota(jnp.int32, (table_width, table_width), 0)
        later = lax.broadcasted_iota(jnp.int32, (table_width, table_width), 1)
        before = jnp.where(earlier < later, 1.0, 0.0).astype(jnp.bfloat16)
        order = lax.broadcasted_iota(jnp.int32, (list_width, table_width), 0)
        line = lax.broadcasted_iota(jnp.int32, (8, table_width), 0)
        for p in range(prompts):
            local = table_ref[p : p + 1, :] - me * page_count
            owned = jnp.where(jnp.logical_and(local >= 0, local < page_count), 1, 0)
            many = jnp.broadcast_to(owned, (8, table_width)).astype(jnp.float32)
            rank = jnp.dot(
                many.astype(jnp.bfloat16), before, preferred_element_type=jnp.float32
            )[0:1].astype(jnp.int32)
            hot = jnp.where(jnp.logical_and(order == rank, owned > 0), 1.0, 0.0)
            left = jnp.minimum(len_ref[p] - column * page_rows, page_rows)
            count = jnp.sum(owned, axis=1, keepdims=True)
            values = jnp.where(line == 0, local * owned, left * owned).astype(jnp.float32)
            picked = lax.dot_general(
                values.astype(jnp.bfloat16), hot.astype(jnp.bfloat16), trans_b,
                preferred_element_type=jnp.float32,
            ).astype(jnp.int32)
            picked_line = lax.broadcasted_iota(jnp.int32, picked.shape, 0)
            list_buf[p] = jnp.where(picked_line == 2, count, picked)

    width = gain_ref.shape[1]
    extra = []
    for d in range(1, major):
        for c in range(2):
            forward_down(d, c)
            forward_up(d, c)
        if d == 1:
            raw_copy.wait()
            raw = raw_mine[...] + raw_other[...]
            latent = raw[:, :width]
            spread = lax.rsqrt(jnp.mean(latent * latent, axis=-1, keepdims=True) + eps)
            done = jnp.concatenate(
                [latent * spread * gain_ref[...], raw[:, width:]], axis=1
            )
            rows_buf[...] = jnp.concatenate([done, jnp.zeros_like(done)], axis=0).astype(
                jnp.bfloat16
            )
            for i in range(per_host):
                new_buf[i] = done[i * steps : (i + 1) * steps].astype(jnp.bfloat16)
            page_lists()
            extra = [
                pltpu.make_async_copy(rows_buf, rows_ref, own_sem.at[2]),
                pltpu.make_async_copy(list_buf, list_ref, own_sem.at[3]),
                pltpu.make_async_copy(new_buf, new_ref, own_sem.at[4]),
            ]
            for copy in extra:
                copy.start()
    for k in range(major):
        for c in range(2):
            await_recv(k * minor + (1 - b), c)
    own_q.wait()
    own_hs.wait()
    for copy in extra:
        copy.wait()
    for k in range(major):
        src = k * minor + b

        @pl.when(jnp.logical_and(a > 0, k >= a))
        def _():
            await_send(src, False, 0, me - minor)

        @pl.when(jnp.logical_and(a < major - 1, k <= a))
        def _():
            await_send(src, False, 1, me + minor)

        await_send(src, False, 2, mate)


def attend_kernel(
    list_ref, hs_ref, q_hbm, fresh_hbm, new_in, pool_ref, up_ref, o_ref, ml_ref, new_out,
    q_ref, fresh_ref, in_sem, kbuf, sbuf, sfresh, qp, acc, oacc, mbuf, lbuf, mlcol, upbuf, slot_of, page_sem, up_sem,
):
    prompts = list_ref.shape[0]
    per_host = 2
    slots, slot_rows, width = q_ref.shape
    heads, latent, vhead = up_ref.shape
    rows = fork_count * slot_rows
    me = lax.axis_index("seq")

    def page_copy(p, i, at):
        return pltpu.make_async_copy(pool_ref.at[list_ref[p, 0, i]], kbuf.at[at], page_sem.at[at])

    def blocks_of(p):
        return (list_ref[p, 2, 0] + block_pages - 1) // block_pages

    def start_prompt(p, base):
        count = blocks_of(p) * block_pages

        def start_page(i, carry):
            page_copy(p, i, base + i).start()
            return carry

        lax.fori_loop(0, count, start_page, 0)
        return base + count

    first = [
        pltpu.make_async_copy(q_hbm, q_ref, in_sem.at[0]),
        pltpu.make_async_copy(fresh_hbm, fresh_ref, in_sem.at[1]),
    ]
    for copy in first:
        copy.start()
    lax.fori_loop(0, prompts, start_prompt, 0)
    new_copy = pltpu.make_async_copy(new_in, new_out, in_sem.at[2])
    new_copy.start()
    up_copy = pltpu.make_async_copy(up_ref, upbuf, up_sem)
    up_copy.start()

    def note_slot(i, carry):
        slot_of[hs_ref[i // per_host, 0, i % per_host]] = i
        return carry

    lax.fori_loop(0, slots, note_slot, 0)
    for copy in first:
        copy.wait()
    lane = lax.broadcasted_iota(jnp.int32, (1, 128), 1)
    fresh_lane = lax.broadcasted_iota(jnp.int32, (slot_rows, 16), 1)
    step_of = lax.broadcasted_iota(jnp.int32, (slot_rows, 16), 0) // heads
    step_ok = jnp.logical_and(fresh_lane % 2 <= step_of, fresh_lane < 2 * per_host)

    def one_prompt(p, base):
        for f in range(fork_count):
            qp[f * slot_rows : (f + 1) * slot_rows, :] = q_ref[slot_of[p * fork_count + f]]
        fresh_all = (
            lax.dot_general(qp[...], fresh_ref[...], trans_b, preferred_element_type=jnp.float32)
            * log2_scale
        )
        for f in range(fork_count):
            part = slice(f * slot_rows, (f + 1) * slot_rows)
            mine = slot_of[p * fork_count + f] - me * per_host
            seen = jnp.logical_and(step_ok, fresh_lane // 2 == mine)
            scores = jnp.where(seen, fresh_all[part], floor_score)
            sfresh[part, :] = scores
            mbuf[part, :] = jnp.broadcast_to(
                jnp.max(scores, axis=1, keepdims=True), (slot_rows, 128)
            )
        blocks = blocks_of(p)

        def score_block(j, carry):
            for i in range(block_pages):
                page_copy(p, j * block_pages + i, base + j * block_pages + i).wait()
            keys = jnp.concatenate(
                [kbuf[base + j * block_pages + i] for i in range(block_pages)], axis=1
            )
            scores = jnp.dot(qp[...], keys, preferred_element_type=jnp.float32) * log2_scale
            top = mbuf[...]
            for i in range(block_pages):
                live = list_ref[p, 1, j * block_pages + i]
                piece = jnp.where(lane < live, scores[:, i * 128 : (i + 1) * 128], floor_score)
                sbuf[j, :, i * 128 : (i + 1) * 128] = piece
                top = jnp.maximum(top, piece)
            mbuf[...] = top
            return carry

        lax.fori_loop(0, blocks, score_block, 0)
        top = jnp.max(mbuf[...], axis=1, keepdims=True)
        mbuf[...] = jnp.broadcast_to(top, (rows, 128))
        fresh_scores = sfresh[...]
        fresh_w = jnp.where(fresh_scores > floor_score, jnp.exp2(fresh_scores - top), 0.0)
        fresh_total = jnp.sum(fresh_w, axis=1, keepdims=True)
        lbuf[...] = jnp.where(lane == 0, fresh_total, 0.0)
        fresh_w = fresh_w.astype(jnp.bfloat16)
        for c in range(latent // 128):
            acc[c] = jnp.dot(
                fresh_w, fresh_ref[:, c * 128 : (c + 1) * 128], preferred_element_type=jnp.float32
            )

        def add_block(j, carry):
            keys = jnp.concatenate(
                [kbuf[base + j * block_pages + i, :latent] for i in range(block_pages)], axis=1
            )
            top = mbuf[...]
            total = lbuf[...]
            rounded = []
            for i in range(block_pages):
                w = jnp.exp2(sbuf[j, :, i * 128 : (i + 1) * 128] - top)
                total = total + w
                rounded.append(w.astype(jnp.bfloat16))
            lbuf[...] = total
            part = lax.dot_general(
                jnp.concatenate(rounded, axis=1), keys, trans_b,
                preferred_element_type=jnp.float32,
            )
            for c in range(latent // 128):
                acc[c] += part[:, c * 128 : (c + 1) * 128]
            return carry

        lax.fori_loop(0, blocks, add_block, 0)
        total = jnp.sum(lbuf[...], axis=1, keepdims=True)
        ml = jnp.where(lane == 0, mbuf[...], total)

        @pl.when(p == 0)
        def _():
            up_copy.wait()

        group = 2 * fork_count
        for h in range(heads):
            x = jnp.concatenate(
                [acc[c, pl.ds(h, group, stride=heads), :] for c in range(latent // 128)], axis=1
            )
            hi = x.astype(jnp.bfloat16)
            lo = (x - hi.astype(jnp.float32)).astype(jnp.bfloat16)
            y = jnp.dot(
                jnp.concatenate([hi, lo], axis=0), upbuf[h], preferred_element_type=jnp.float32
            )
            oacc[pl.ds(h, group, stride=heads), :] = y[:group] + y[group:]
        for f in range(fork_count):
            part = slice(f * slot_rows, (f + 1) * slot_rows)
            slot = slot_of[p * fork_count + f]
            o_ref[slot] = oacc[part, :]
            mlcol[slot] = ml[part]
        return base + blocks * block_pages

    lax.fori_loop(0, prompts, one_prompt, 0)

    def turn(d, carry):
        both = mlcol[pl.ds(d * per_host, per_host)].reshape(per_host * slot_rows, 128)
        ml_ref[d] = both.T[0:8]
        return carry

    lax.fori_loop(0, slots // per_host, turn, 0)
    new_copy.wait()


def combine_kernel(
    n, o_ref, ml_ref, out_ref, o_got, ml_got, gains, o_send, o_recv, ml_send, ml_recv
):
    me = lax.axis_index("seq")
    barrier = pltpu.get_barrier_semaphore()
    for k in range(1, n):
        pl.semaphore_signal(
            barrier, inc=1, device_id={"seq": (me + k) % n}, device_id_type=mesh_ids
        )
    pl.semaphore_wait(barrier, n - 1)
    copies = []
    for k in range(1, n):
        dest = (me + k) % n
        for src, got, s_sem, r_sem in (
            (ml_ref, ml_got, ml_send, ml_recv),
            (o_ref, o_got, o_send, o_recv),
        ):
            copy = pltpu.make_async_remote_copy(
                src_ref=src.at[dest],
                dst_ref=got.at[k],
                send_sem=s_sem.at[k],
                recv_sem=r_sem.at[k],
                device_id={"seq": dest},
                device_id_type=mesh_ids,
            )
            copy.start()
            copies.append(copy)
    ml_got[0] = ml_ref[me]
    o_got[0] = o_ref[me]
    for copy in copies:
        copy.wait()
    top = ml_got[0, 0:1, :]
    for k in range(1, n):
        top = jnp.maximum(top, ml_got[k, 0:1, :])
    total = jnp.zeros_like(top)
    gains[...] = jnp.zeros_like(gains)
    for k in range(n):
        factor = jnp.exp2(ml_got[k, 0:1, :] - top)
        gains[k : k + 1, :] = factor
        total = total + factor * ml_got[k, 1:2, :]
    turned = (gains[...] / total).T
    out = turned[:, 0:1] * o_got[0]
    for k in range(1, n):
        out = out + turned[:, k : k + 1] * o_got[k]
    out_ref[...] = out.astype(jnp.bfloat16)


def attend(lists, hsall, qall, rows16, new_rows, pool, value_up):
    n = hsall.shape[0]
    prompts = lists.shape[0]
    slots, slot_rows, width = qall.shape
    heads, latent, vhead = value_up.shape
    page_count, page_rows = pool.shape[0], pool.shape[2]
    rows = fork_count * slot_rows
    score_blocks = -(-page_count // block_pages)
    slots_held = score_blocks * block_pages + (block_pages - 1) * prompts
    return pl.pallas_call(
        attend_kernel,
        out_shape=(
            jax.ShapeDtypeStruct((slots, slot_rows, vhead), jnp.float32),
            jax.ShapeDtypeStruct((n, 8, 128), jnp.float32),
            jax.ShapeDtypeStruct(new_rows.shape, jnp.bfloat16),
        ),
        in_specs=[smem, smem, hbm, hbm, hbm, hbm, hbm],
        out_specs=(vmem, vmem, hbm),
        scratch_shapes=[
            pltpu.VMEM((slots, slot_rows, width), jnp.bfloat16),
            pltpu.VMEM((16, width), jnp.bfloat16),
            pltpu.SemaphoreType.DMA((3,)),
            pltpu.VMEM((slots_held, width, page_rows), jnp.bfloat16),
            pltpu.VMEM((score_blocks, rows, block_pages * page_rows), jnp.float32),
            pltpu.VMEM((rows, 16), jnp.float32),
            pltpu.VMEM((rows, width), jnp.bfloat16),
            pltpu.VMEM((latent // 128, rows, 128), jnp.float32),
            pltpu.VMEM((rows, vhead), jnp.float32),
            pltpu.VMEM((rows, 128), jnp.float32),
            pltpu.VMEM((rows, 128), jnp.float32),
            pltpu.VMEM((slots, slot_rows, 128), jnp.float32),
            pltpu.VMEM(value_up.shape, jnp.bfloat16),
            pltpu.SMEM((slots,), jnp.int32),
            pltpu.SemaphoreType.DMA((slots_held,)),
            pltpu.SemaphoreType.DMA,
        ],
        compiler_params=pltpu.CompilerParams(vmem_limit_bytes=60 * 2**20),
    )(lists, hsall, qall, rows16, new_rows, pool, value_up)


def on_device(
    cache_pool, page_table, prompt_len, host_samples, queries, new_hidden, kv_down, kv_gain,
    value_up,
):
    n = lax.axis_size("seq")
    big = pltpu.CompilerParams
    per_host, steps, heads, width = queries.shape
    latent = kv_gain.shape[0]
    vhead = value_up.shape[2]
    page_count, page_rows = cache_pool.shape[:2]
    prompts = page_table.shape[0]
    host_rows = per_host * steps * heads
    slot_rows = steps * heads
    slots = n * per_host
    rows = fork_count * slot_rows
    list_width = -(-page_count // 128) * 128
    qall, hsall, rows16, new_rows, lists = pl.pallas_call(
        functools.partial(gather_kernel, n, page_count, page_rows),
        out_shape=(
            jax.ShapeDtypeStruct((n, host_rows, width), jnp.bfloat16),
            jax.ShapeDtypeStruct((n, 8, 128), jnp.int32),
            jax.ShapeDtypeStruct((16, width), jnp.bfloat16),
            jax.ShapeDtypeStruct((per_host, steps, width), jnp.bfloat16),
            jax.ShapeDtypeStruct((prompts, 8, list_width), jnp.int32),
        ),
        in_specs=[hbm, smem, hbm, hbm, hbm, hbm, smem],
        out_specs=(hbm, hbm, hbm, hbm, hbm),
        scratch_shapes=[
            pltpu.VMEM(kv_down.shape[::-1], jnp.bfloat16),
            pltpu.VMEM(new_hidden.shape, jnp.bfloat16),
            pltpu.VMEM((1, latent), jnp.float32),
            pltpu.VMEM(page_table.shape, jnp.int32),
            pltpu.VMEM((8, width), jnp.float32),
            pltpu.VMEM((8, width), jnp.float32),
            pltpu.VMEM((8, kv_down.shape[0]), jnp.float32),
            pltpu.VMEM((8, 128), jnp.int32),
            pltpu.VMEM((16, width), jnp.bfloat16),
            pltpu.VMEM((per_host, steps, width), jnp.bfloat16),
            pltpu.VMEM((prompts, 8, list_width), jnp.int32),
            pltpu.SemaphoreType.DMA,
            pltpu.SemaphoreType.DMA((8,)),
            pltpu.SemaphoreType.DMA((n, 3, 2)),
            pltpu.SemaphoreType.DMA((n, 2)),
            pltpu.SemaphoreType.DMA((n, 3)),
            pltpu.SemaphoreType.DMA((n,)),
            pltpu.SemaphoreType.DMA,
            pltpu.SemaphoreType.DMA,
        ],
        compiler_params=big(
            collective_id=0, has_side_effects=True, vmem_limit_bytes=62 * 2**20
        ),
    )(
        queries.reshape(host_rows, width), host_samples, new_hidden, kv_down.T, kv_gain[None, :],
        page_table, prompt_len,
    )

    o, ml, new_rows = attend(
        lists, hsall, qall.reshape(slots, slot_rows, width), rows16, new_rows,
        jnp.swapaxes(cache_pool, 1, 2), value_up,
    )

    out = pl.pallas_call(
        functools.partial(combine_kernel, n),
        out_shape=jax.ShapeDtypeStruct((host_rows, vhead), jnp.bfloat16),
        in_specs=[vmem, vmem],
        out_specs=vmem,
        scratch_shapes=[
            pltpu.VMEM((n, host_rows, vhead), jnp.float32),
            pltpu.VMEM((n, 8, 128), jnp.float32),
            pltpu.VMEM((128, 128), jnp.float32),
            pltpu.SemaphoreType.DMA((n,)),
            pltpu.SemaphoreType.DMA((n,)),
            pltpu.SemaphoreType.DMA((n,)),
            pltpu.SemaphoreType.DMA((n,)),
        ],
        compiler_params=big(
            collective_id=1, has_side_effects=True, vmem_limit_bytes=16 * 2**20
        ),
    )(o.reshape(n, host_rows, vhead), ml)
    return (new_rows, out.reshape(per_host, steps, heads, vhead))


def solution(mesh):
    in_specs = (
        P(("groups", "seq"), None, None),
        P("groups", None),
        P("groups"),
        P(("groups", "seq")),
        P(("groups", "seq"), None, "head", None),
        P(("groups", "seq"), None, "head"),
        P("head", None),
        P(),
        P("head", None, None),
    )
    out_specs = (P(("groups", "seq"), None, None), P(("groups", "seq"), None, "head", None))
    return jax.shard_map(
        on_device, mesh=mesh, in_specs=in_specs, out_specs=out_specs, check_vma=False
    )
```

```python
import functools

import jax
import jax.numpy as jnp
from jax import lax
from jax.experimental import pallas as pl
from jax.experimental.pallas import tpu as pltpu
from jax.sharding import PartitionSpec as P

eps = 1e-06
log2_scale = 192.0 ** (-0.5) * 1.4426950408889634
floor_score = -1e30
block_pages = 4
fork_count = 8
mesh_ids = pl.DeviceIdType.MESH
vmem = pl.BlockSpec(memory_space=pltpu.VMEM)
smem = pl.BlockSpec(memory_space=pltpu.SMEM)
hbm = pl.BlockSpec(memory_space=pltpu.HBM)
trans_b = (((1,), (1,)), ((), ()))


def gather_kernel(
    n, page_count, page_rows, q_ref, host_ref, nh_hbm, down_ref, gain_hbm, table_hbm, len_ref,
    qall_ref, hsall_ref, rows_ref, new_ref, list_ref,
    down_buf, nh_ref, gain_ref, table_ref, raw_mine, raw_other, nh_buf, hs_ref, rows_buf, new_buf, list_buf, down_sem, own_sem, q_send,
    q_recv, hs_send, hs_recv, raw_send, raw_recv,
):
    minor = 2
    major = n // minor
    me = lax.axis_index("seq")
    a, b = me // minor, me % minor
    head = lax.axis_index("head")
    half = q_ref.shape[0] // 2
    down_copy = pltpu.make_async_copy(down_ref, down_buf, down_sem)
    small = []
    for i, (source, target) in enumerate(
        ((nh_hbm, nh_ref), (gain_hbm, gain_ref), (table_hbm, table_ref))
    ):
        copy = pltpu.make_async_copy(source, target, own_sem.at[5 + i])
        copy.start()
        small.append(copy)
    down_copy.start()
    barrier = pltpu.get_barrier_semaphore()

    def greet(where):
        pl.semaphore_signal(barrier, inc=1, device_id=where, device_id_type=mesh_ids)

    @pl.when(a > 0)
    def _():
        greet({"seq": me - minor})

    @pl.when(a < major - 1)
    def _():
        greet({"seq": me + minor})

    mate = a * minor + (1 - b)
    greet({"seq": mate})
    greet({"head": 1 - head})
    lane = lax.broadcasted_iota(jnp.int32, (8, 128), 1)
    tile = jnp.zeros((8, 128), jnp.int32)
    for i in range(host_ref.shape[0]):
        tile = jnp.where(lane == i, host_ref[i], tile)
    hs_ref[...] = tile
    near = jnp.where(a > 0, 1, 0) + jnp.where(a < major - 1, 1, 0)
    pl.semaphore_wait(barrier, 2 + near)

    def copies(src, c, first, way, dest):
        rows = pl.ds(c * half, half)
        found = [
            pltpu.make_async_remote_copy(
                src_ref=q_ref.at[rows] if first else qall_ref.at[src, rows],
                dst_ref=qall_ref.at[src, rows],
                send_sem=q_send.at[src, way, c],
                recv_sem=q_recv.at[src, c],
                device_id={"seq": dest},
                device_id_type=mesh_ids,
            )
        ]
        if c == 0:
            found.append(
                pltpu.make_async_remote_copy(
                    src_ref=hs_ref if first else hsall_ref.at[src],
                    dst_ref=hsall_ref.at[src],
                    send_sem=hs_send.at[src, way],
                    recv_sem=hs_recv.at[src],
                    device_id={"seq": dest},
                    device_id_type=mesh_ids,
                )
            )
        return found

    def send(src, c, first, way, dest):
        for copy in copies(src, c, first, way, dest):
            copy.start()

    def await_send(src, first, way, dest):
        for c in range(2):
            for copy in copies(src, c, first, way, dest):
                copy.wait_send()

    def await_recv(src, c):
        for copy in copies(src, c, False, 0, me):
            copy.wait_recv()

    for c in range(2):

        @pl.when(a > 0)
        def _():
            send(me, c, True, 0, me - minor)

        @pl.when(a < major - 1)
        def _():
            send(me, c, True, 1, me + minor)

        send(me, c, True, 2, mate)
    own_q = pltpu.make_async_copy(q_ref, qall_ref.at[me], own_sem.at[0])
    own_hs = pltpu.make_async_copy(hs_ref, hsall_ref.at[me], own_sem.at[1])
    own_q.start()
    own_hs.start()
    per_host, steps = nh_ref.shape[:2]
    for copy in small:
        copy.wait()
    nh_buf[...] = jnp.zeros_like(nh_buf)
    for i in range(per_host):
        nh_buf[i * steps : (i + 1) * steps, :] = nh_ref[i].astype(jnp.float32)
    down_copy.wait()
    raw_mine[...] = lax.dot_general(
        nh_buf[...].astype(jnp.bfloat16), down_buf[...], trans_b,
        preferred_element_type=jnp.float32,
    )
    raw_copy = pltpu.make_async_remote_copy(
        src_ref=raw_mine,
        dst_ref=raw_other,
        send_sem=raw_send,
        recv_sem=raw_recv,
        device_id={"head": 1 - head},
        device_id_type=mesh_ids,
    )
    raw_copy.start()

    def forward_down(d, c):
        src = me + d * minor

        @pl.when(a + d < major)
        def _():
            await_recv(src, c)

            @pl.when(a > 0)
            def _():
                send(src, c, False, 0, me - minor)

            send(src, c, False, 2, mate)

    def forward_up(d, c):
        src = me - d * minor

        @pl.when(a - d >= 0)
        def _():
            await_recv(src, c)

            @pl.when(a < major - 1)
            def _():
                send(src, c, False, 1, me + minor)

            send(src, c, False, 2, mate)

    def page_lists():
        prompts, table_width = table_ref.shape
        list_width = list_buf.shape[2]
        column = lax.broadcasted_iota(jnp.int32, (1, table_width), 1)
        earlier = lax.broadcasted_iota(jnp.int32, (table_width, table_width), 0)
        later = lax.broadcasted_iota(jnp.int32, (table_width, table_width), 1)
        before = jnp.where(earlier < later, 1.0, 0.0).astype(jnp.bfloat16)
        order = lax.broadcasted_iota(jnp.int32, (list_width, table_width), 0)
        line = lax.broadcasted_iota(jnp.int32, (8, table_width), 0)
        for p in range(prompts):
            local = table_ref[p : p + 1, :] - me * page_count
            owned = jnp.where(jnp.logical_and(local >= 0, local < page_count), 1, 0)
            many = jnp.broadcast_to(owned, (8, table_width)).astype(jnp.float32)
            rank = jnp.dot(
                many.astype(jnp.bfloat16), before, preferred_element_type=jnp.float32
            )[0:1].astype(jnp.int32)
            hot = jnp.where(jnp.logical_and(order == rank, owned > 0), 1.0, 0.0)
            left = jnp.minimum(len_ref[p] - column * page_rows, page_rows)
            count = jnp.sum(owned, axis=1, keepdims=True)
            values = jnp.where(line == 0, local * owned, left * owned).astype(jnp.float32)
            picked = lax.dot_general(
                values.astype(jnp.bfloat16), hot.astype(jnp.bfloat16), trans_b,
                preferred_element_type=jnp.float32,
            ).astype(jnp.int32)
            picked_line = lax.broadcasted_iota(jnp.int32, picked.shape, 0)
            list_buf[p] = jnp.where(picked_line == 2, count, picked)

    width = gain_ref.shape[1]
    extra = []
    for d in range(1, major):
        for c in range(2):
            forward_down(d, c)
            forward_up(d, c)
        if d == 1:
            raw_copy.wait()
            raw = raw_mine[...] + raw_other[...]
            latent = raw[:, :width]
            spread = lax.rsqrt(jnp.mean(latent * latent, axis=-1, keepdims=True) + eps)
            done = jnp.concatenate(
                [latent * spread * gain_ref[...], raw[:, width:]], axis=1
            )
            rows_buf[...] = jnp.concatenate([done, jnp.zeros_like(done)], axis=0).astype(
                jnp.bfloat16
            )
            for i in range(per_host):
                new_buf[i] = done[i * steps : (i + 1) * steps].astype(jnp.bfloat16)
            page_lists()
            extra = [
                pltpu.make_async_copy(rows_buf, rows_ref, own_sem.at[2]),
                pltpu.make_async_copy(list_buf, list_ref, own_sem.at[3]),
                pltpu.make_async_copy(new_buf, new_ref, own_sem.at[4]),
            ]
            for copy in extra:
                copy.start()
    for k in range(major):
        for c in range(2):
            await_recv(k * minor + (1 - b), c)
    own_q.wait()
    own_hs.wait()
    for copy in extra:
        copy.wait()
    for k in range(major):
        src = k * minor + b

        @pl.when(jnp.logical_and(a > 0, k >= a))
        def _():
            await_send(src, False, 0, me - minor)

        @pl.when(jnp.logical_and(a < major - 1, k <= a))
        def _():
            await_send(src, False, 1, me + minor)

        await_send(src, False, 2, mate)


def attend_kernel(
    list_ref, hs_ref, q_hbm, fresh_hbm, new_in, pool_ref, up_ref, o_ref, ml_ref, new_out,
    q_ref, fresh_ref, in_sem, kbuf, sbuf, sfresh, qp, acc, oacc, mbuf, lbuf, mlcol, upbuf, slot_of, page_sem, up_sem,
):
    prompts = list_ref.shape[0]
    per_host = 2
    slots, slot_rows, width = q_ref.shape
    heads, latent, vhead = up_ref.shape
    rows = fork_count * slot_rows
    me = lax.axis_index("seq")

    def page_copy(p, i, at):
        return pltpu.make_async_copy(pool_ref.at[list_ref[p, 0, i]], kbuf.at[at], page_sem.at[at])

    def blocks_of(p):
        return (list_ref[p, 2, 0] + block_pages - 1) // block_pages

    def start_prompt(p, base):
        count = blocks_of(p) * block_pages

        def start_page(i, carry):
            page_copy(p, i, base + i).start()
            return carry

        lax.fori_loop(0, count, start_page, 0)
        return base + count

    first = [
        pltpu.make_async_copy(q_hbm, q_ref, in_sem.at[0]),
        pltpu.make_async_copy(fresh_hbm, fresh_ref, in_sem.at[1]),
    ]
    for copy in first:
        copy.start()
    lax.fori_loop(0, prompts, start_prompt, 0)
    new_copy = pltpu.make_async_copy(new_in, new_out, in_sem.at[2])
    new_copy.start()
    up_copy = pltpu.make_async_copy(up_ref, upbuf, up_sem)
    up_copy.start()

    def note_slot(i, carry):
        slot_of[hs_ref[i // per_host, 0, i % per_host]] = i
        return carry

    lax.fori_loop(0, slots, note_slot, 0)
    for copy in first:
        copy.wait()
    lane = lax.broadcasted_iota(jnp.int32, (1, 128), 1)
    fresh_lane = lax.broadcasted_iota(jnp.int32, (slot_rows, 16), 1)
    step_of = lax.broadcasted_iota(jnp.int32, (slot_rows, 16), 0) // heads
    step_ok = jnp.logical_and(fresh_lane % 2 <= step_of, fresh_lane < 2 * per_host)

    def one_prompt(p, base):
        for f in range(fork_count):
            qp[f * slot_rows : (f + 1) * slot_rows, :] = q_ref[slot_of[p * fork_count + f]]
        fresh_all = (
            lax.dot_general(qp[...], fresh_ref[...], trans_b, preferred_element_type=jnp.float32)
            * log2_scale
        )
        for f in range(fork_count):
            part = slice(f * slot_rows, (f + 1) * slot_rows)
            mine = slot_of[p * fork_count + f] - me * per_host
            seen = jnp.logical_and(step_ok, fresh_lane // 2 == mine)
            scores = jnp.where(seen, fresh_all[part], floor_score)
            sfresh[part, :] = scores
            mbuf[part, :] = jnp.broadcast_to(
                jnp.max(scores, axis=1, keepdims=True), (slot_rows, 128)
            )
        blocks = blocks_of(p)

        def score_block(j, carry):
            for i in range(block_pages):
                page_copy(p, j * block_pages + i, base + j * block_pages + i).wait()
            keys = jnp.concatenate(
                [kbuf[base + j * block_pages + i] for i in range(block_pages)], axis=1
            )
            scores = jnp.dot(qp[...], keys, preferred_element_type=jnp.float32) * log2_scale
            top = mbuf[...]
            for i in range(block_pages):
                live = list_ref[p, 1, j * block_pages + i]
                piece = jnp.where(lane < live, scores[:, i * 128 : (i + 1) * 128], floor_score)
                sbuf[j, :, i * 128 : (i + 1) * 128] = piece
                top = jnp.maximum(top, piece)
            mbuf[...] = top
            return carry

        lax.fori_loop(0, blocks, score_block, 0)
        top = jnp.max(mbuf[...], axis=1, keepdims=True)
        mbuf[...] = jnp.broadcast_to(top, (rows, 128))
        fresh_scores = sfresh[...]
        fresh_w = jnp.where(fresh_scores > floor_score, jnp.exp2(fresh_scores - top), 0.0)
        fresh_total = jnp.sum(fresh_w, axis=1, keepdims=True)
        lbuf[...] = jnp.where(lane == 0, fresh_total, 0.0)
        fresh_w = fresh_w.astype(jnp.bfloat16)
        for c in range(latent // 128):
            acc[c] = jnp.dot(
                fresh_w, fresh_ref[:, c * 128 : (c + 1) * 128], preferred_element_type=jnp.float32
            )

        def add_block(j, carry):
            keys = jnp.concatenate(
                [kbuf[base + j * block_pages + i, :latent] for i in range(block_pages)], axis=1
            )
            top = mbuf[...]
            total = lbuf[...]
            rounded = []
            for i in range(block_pages):
                w = jnp.exp2(sbuf[j, :, i * 128 : (i + 1) * 128] - top)
                total = total + w
                rounded.append(w.astype(jnp.bfloat16))
            lbuf[...] = total
            part = lax.dot_general(
                jnp.concatenate(rounded, axis=1), keys, trans_b,
                preferred_element_type=jnp.float32,
            )
            for c in range(latent // 128):
                acc[c] += part[:, c * 128 : (c + 1) * 128]
            return carry

        lax.fori_loop(0, blocks, add_block, 0)
        total = jnp.sum(lbuf[...], axis=1, keepdims=True)
        ml = jnp.where(lane == 0, mbuf[...], total)

        @pl.when(p == 0)
        def _():
            up_copy.wait()

        group = 2 * fork_count
        for h in range(heads):
            x = jnp.concatenate(
                [acc[c, pl.ds(h, group, stride=heads), :] for c in range(latent // 128)], axis=1
            )
            hi = x.astype(jnp.bfloat16)
            lo = (x - hi.astype(jnp.float32)).astype(jnp.bfloat16)
            y = jnp.dot(
                jnp.concatenate([hi, lo], axis=0), upbuf[h], preferred_element_type=jnp.float32
            )
            oacc[pl.ds(h, group, stride=heads), :] = y[:group] + y[group:]
        for f in range(fork_count):
            part = slice(f * slot_rows, (f + 1) * slot_rows)
            slot = slot_of[p * fork_count + f]
            o_ref[slot] = oacc[part, :]
            mlcol[slot] = ml[part]
        return base + blocks * block_pages

    lax.fori_loop(0, prompts, one_prompt, 0)

    def turn(d, carry):
        both = mlcol[pl.ds(d * per_host, per_host)].reshape(per_host * slot_rows, 128)
        ml_ref[d] = both.T[0:8]
        return carry

    lax.fori_loop(0, slots // per_host, turn, 0)
    new_copy.wait()


def merge(blocks, ml_of, o_of, gains):
    top = ml_of(0)[0:1]
    for k in range(1, blocks):
        top = jnp.maximum(top, ml_of(k)[0:1])
    total = jnp.zeros_like(top)
    gains[...] = jnp.zeros_like(gains)
    for k in range(blocks):
        factor = jnp.exp2(ml_of(k)[0:1] - top)
        gains[k : k + 1, :] = factor
        total = total + factor * ml_of(k)[1:2]
    return top, total


def weigh(blocks, turned, o_of):
    out = turned[:, 0:1] * o_of(0)
    for k in range(1, blocks):
        out = out + turned[:, k : k + 1] * o_of(k)
    return out


def combine_kernel(
    n, o_ref, ml_ref, out_ref, o_own, ml_own, o_mate, ml_mate, o_pair, ml_pair, o_got, ml_got,
    gains, own_sem, mate_send, mate_recv, far_send, far_recv,
):
    minor = 2
    major = n // minor
    me = lax.axis_index("seq")
    a, b = me // minor, me % minor
    mate = a * minor + (1 - b)
    barrier = pltpu.get_barrier_semaphore()
    pl.semaphore_signal(barrier, inc=1, device_id={"seq": mate}, device_id_type=mesh_ids)
    for k in range(1, major):
        pl.semaphore_signal(
            barrier, inc=1, device_id={"seq": (me + k * minor) % n}, device_id_type=mesh_ids
        )
    order = list(range(1, major)) + [0]
    owns = []
    for k in order:
        place = (a + k) % major * minor + b
        pair = [
            pltpu.make_async_copy(ml_ref.at[place], ml_own.at[k], own_sem.at[k, 0]),
            pltpu.make_async_copy(o_ref.at[place], o_own.at[k], own_sem.at[k, 1]),
        ]
        for copy in pair:
            copy.start()
        owns.append(pair)
    pl.semaphore_wait(barrier, major)

    def push(src, dst, sems, k, i, dest):
        copy = pltpu.make_async_remote_copy(
            src_ref=src,
            dst_ref=dst,
            send_sem=sems[0].at[k, i],
            recv_sem=sems[1].at[k, i],
            device_id={"seq": dest},
            device_id_type=mesh_ids,
        )
        copy.start()
        return copy

    near = (mate_send, mate_recv)
    far = (far_send, far_recv)
    swaps = []
    for k in order:
        place = (a + k) % major * minor + (1 - b)
        swaps.append(
            [
                push(ml_ref.at[place], ml_mate.at[k], near, k, 0, mate),
                push(o_ref.at[place], o_mate.at[k], near, k, 1, mate),
            ]
        )
    sent = []
    line = lax.broadcasted_iota(jnp.int32, (8, 128), 0)
    for at, k in enumerate(order):
        for copy in owns[at]:
            copy.wait()
        for copy in swaps[at]:
            copy.wait_recv()
        ml_of = lambda i: (ml_own if i == 0 else ml_mate)[k]
        o_of = lambda i: (o_own if i == 0 else o_mate)[k]
        top, total = merge(2, ml_of, o_of, gains)
        summed = weigh(2, gains[...].T, o_of)
        both = jnp.where(line == 0, top, total)
        if k == 0:
            ml_got[0] = both
            o_got[0] = summed
        else:
            ml_pair[k] = both
            o_pair[k] = summed
            dest = (me + k * minor) % n
            sent.append(push(ml_pair.at[k], ml_got.at[k], far, k, 0, dest))
            sent.append(push(o_pair.at[k], o_got.at[k], far, k, 1, dest))
    for copy in sent:
        copy.wait_recv()
    top, total = merge(major, lambda i: ml_got[i], lambda i: o_got[i], gains)
    out = weigh(major, (gains[...] / total).T, lambda i: o_got[i])
    out_ref[...] = out.astype(jnp.bfloat16)
    for pair in swaps:
        for copy in pair:
            copy.wait_send()
    for copy in sent:
        copy.wait_send()


def attend(lists, hsall, qall, rows16, new_rows, pool, value_up):
    n = hsall.shape[0]
    prompts = lists.shape[0]
    slots, slot_rows, width = qall.shape
    heads, latent, vhead = value_up.shape
    page_count, page_rows = pool.shape[0], pool.shape[2]
    rows = fork_count * slot_rows
    score_blocks = -(-page_count // block_pages)
    slots_held = score_blocks * block_pages + (block_pages - 1) * prompts
    return pl.pallas_call(
        attend_kernel,
        out_shape=(
            jax.ShapeDtypeStruct((slots, slot_rows, vhead), jnp.float32),
            jax.ShapeDtypeStruct((n, 8, 128), jnp.float32),
            jax.ShapeDtypeStruct(new_rows.shape, jnp.bfloat16),
        ),
        in_specs=[smem, smem, hbm, hbm, hbm, hbm, hbm],
        out_specs=(vmem, vmem, hbm),
        scratch_shapes=[
            pltpu.VMEM((slots, slot_rows, width), jnp.bfloat16),
            pltpu.VMEM((16, width), jnp.bfloat16),
            pltpu.SemaphoreType.DMA((3,)),
            pltpu.VMEM((slots_held, width, page_rows), jnp.bfloat16),
            pltpu.VMEM((score_blocks, rows, block_pages * page_rows), jnp.float32),
            pltpu.VMEM((rows, 16), jnp.float32),
            pltpu.VMEM((rows, width), jnp.bfloat16),
            pltpu.VMEM((latent // 128, rows, 128), jnp.float32),
            pltpu.VMEM((rows, vhead), jnp.float32),
            pltpu.VMEM((rows, 128), jnp.float32),
            pltpu.VMEM((rows, 128), jnp.float32),
            pltpu.VMEM((slots, slot_rows, 128), jnp.float32),
            pltpu.VMEM(value_up.shape, jnp.bfloat16),
            pltpu.SMEM((slots,), jnp.int32),
            pltpu.SemaphoreType.DMA((slots_held,)),
            pltpu.SemaphoreType.DMA,
        ],
        compiler_params=pltpu.CompilerParams(vmem_limit_bytes=60 * 2**20),
    )(lists, hsall, qall, rows16, new_rows, pool, value_up)


def on_device(
    cache_pool, page_table, prompt_len, host_samples, queries, new_hidden, kv_down, kv_gain,
    value_up,
):
    n = lax.axis_size("seq")
    big = pltpu.CompilerParams
    per_host, steps, heads, width = queries.shape
    latent = kv_gain.shape[0]
    vhead = value_up.shape[2]
    page_count, page_rows = cache_pool.shape[:2]
    prompts = page_table.shape[0]
    host_rows = per_host * steps * heads
    slot_rows = steps * heads
    slots = n * per_host
    rows = fork_count * slot_rows
    list_width = -(-page_count // 128) * 128
    qall, hsall, rows16, new_rows, lists = pl.pallas_call(
        functools.partial(gather_kernel, n, page_count, page_rows),
        out_shape=(
            jax.ShapeDtypeStruct((n, host_rows, width), jnp.bfloat16),
            jax.ShapeDtypeStruct((n, 8, 128), jnp.int32),
            jax.ShapeDtypeStruct((16, width), jnp.bfloat16),
            jax.ShapeDtypeStruct((per_host, steps, width), jnp.bfloat16),
            jax.ShapeDtypeStruct((prompts, 8, list_width), jnp.int32),
        ),
        in_specs=[hbm, smem, hbm, hbm, hbm, hbm, smem],
        out_specs=(hbm, hbm, hbm, hbm, hbm),
        scratch_shapes=[
            pltpu.VMEM(kv_down.shape[::-1], jnp.bfloat16),
            pltpu.VMEM(new_hidden.shape, jnp.bfloat16),
            pltpu.VMEM((1, latent), jnp.float32),
            pltpu.VMEM(page_table.shape, jnp.int32),
            pltpu.VMEM((8, width), jnp.float32),
            pltpu.VMEM((8, width), jnp.float32),
            pltpu.VMEM((8, kv_down.shape[0]), jnp.float32),
            pltpu.VMEM((8, 128), jnp.int32),
            pltpu.VMEM((16, width), jnp.bfloat16),
            pltpu.VMEM((per_host, steps, width), jnp.bfloat16),
            pltpu.VMEM((prompts, 8, list_width), jnp.int32),
            pltpu.SemaphoreType.DMA,
            pltpu.SemaphoreType.DMA((8,)),
            pltpu.SemaphoreType.DMA((n, 3, 2)),
            pltpu.SemaphoreType.DMA((n, 2)),
            pltpu.SemaphoreType.DMA((n, 3)),
            pltpu.SemaphoreType.DMA((n,)),
            pltpu.SemaphoreType.DMA,
            pltpu.SemaphoreType.DMA,
        ],
        compiler_params=big(
            collective_id=0, has_side_effects=True, vmem_limit_bytes=62 * 2**20
        ),
    )(
        queries.reshape(host_rows, width), host_samples, new_hidden, kv_down.T, kv_gain[None, :],
        page_table, prompt_len,
    )

    o, ml, new_rows = attend(
        lists, hsall, qall.reshape(slots, slot_rows, width), rows16, new_rows,
        jnp.swapaxes(cache_pool, 1, 2), value_up,
    )

    out = pl.pallas_call(
        functools.partial(combine_kernel, n),
        out_shape=jax.ShapeDtypeStruct((host_rows, vhead), jnp.bfloat16),
        in_specs=[hbm, hbm],
        out_specs=vmem,
        scratch_shapes=[
            pltpu.VMEM((n // 2, lines, 128), jnp.float32)
            for _ in range(4)
            for lines in (host_rows, 8)
        ]
        + [
            pltpu.VMEM((128, 128), jnp.float32),
            pltpu.SemaphoreType.DMA((n // 2, 2)),
            pltpu.SemaphoreType.DMA((n // 2, 2)),
            pltpu.SemaphoreType.DMA((n // 2, 2)),
            pltpu.SemaphoreType.DMA((n // 2, 2)),
            pltpu.SemaphoreType.DMA((n // 2, 2)),
        ],
        compiler_params=big(
            collective_id=1, has_side_effects=True, vmem_limit_bytes=62 * 2**20
        ),
    )(o.reshape(n, host_rows, vhead), ml)
    return (new_rows, out.reshape(per_host, steps, heads, vhead))


def solution(mesh):
    in_specs = (
        P(("groups", "seq"), None, None),
        P("groups", None),
        P("groups"),
        P(("groups", "seq")),
        P(("groups", "seq"), None, "head", None),
        P(("groups", "seq"), None, "head"),
        P("head", None),
        P(),
        P("head", None, None),
    )
    out_specs = (P(("groups", "seq"), None, None), P(("groups", "seq"), None, "head", None))
    return jax.shard_map(
        on_device, mesh=mesh, in_specs=in_specs, out_specs=out_specs, check_vma=False
    )
```

```python
import functools

import jax
import jax.numpy as jnp
from jax import lax
from jax.experimental import pallas as pl
from jax.experimental.pallas import tpu as pltpu
from jax.sharding import PartitionSpec as P

eps = 1e-06
log2_scale = 192.0 ** (-0.5) * 1.4426950408889634
floor_score = -1e30
block_pages = 4
fork_count = 8
mesh_ids = pl.DeviceIdType.MESH
vmem = pl.BlockSpec(memory_space=pltpu.VMEM)
smem = pl.BlockSpec(memory_space=pltpu.SMEM)
hbm = pl.BlockSpec(memory_space=pltpu.HBM)
trans_b = (((1,), (1,)), ((), ()))


def gather_kernel(
    n, page_count, page_rows, q_ref, host_ref, nh_hbm, down_ref, gain_hbm, table_hbm, len_ref,
    qall_ref, hsall_ref, rows_ref, new_ref, list_ref,
    down_buf, nh_ref, gain_ref, table_ref, raw_mine, raw_other, nh_buf, hs_ref, rows_buf, new_buf, list_buf, down_sem, own_sem, q_send,
    q_recv, hs_send, hs_recv, raw_send, raw_recv,
):
    minor = 2
    major = n // minor
    me = lax.axis_index("seq")
    a, b = me // minor, me % minor
    head = lax.axis_index("head")
    half = q_ref.shape[0] // 2
    down_copy = pltpu.make_async_copy(down_ref, down_buf, down_sem)
    small = []
    for i, (source, target) in enumerate(
        ((nh_hbm, nh_ref), (gain_hbm, gain_ref), (table_hbm, table_ref))
    ):
        copy = pltpu.make_async_copy(source, target, own_sem.at[5 + i])
        copy.start()
        small.append(copy)
    down_copy.start()
    barrier = pltpu.get_barrier_semaphore()

    def greet(where):
        pl.semaphore_signal(barrier, inc=1, device_id=where, device_id_type=mesh_ids)

    @pl.when(a > 0)
    def _():
        greet({"seq": me - minor})

    @pl.when(a < major - 1)
    def _():
        greet({"seq": me + minor})

    mate = a * minor + (1 - b)
    greet({"seq": mate})
    greet({"head": 1 - head})
    lane = lax.broadcasted_iota(jnp.int32, (8, 128), 1)
    tile = jnp.zeros((8, 128), jnp.int32)
    for i in range(host_ref.shape[0]):
        tile = jnp.where(lane == i, host_ref[i], tile)
    hs_ref[...] = tile
    near = jnp.where(a > 0, 1, 0) + jnp.where(a < major - 1, 1, 0)
    pl.semaphore_wait(barrier, 2 + near)

    def copies(src, c, first, way, dest):
        rows = pl.ds(c * half, half)
        found = [
            pltpu.make_async_remote_copy(
                src_ref=q_ref.at[rows] if first else qall_ref.at[src, rows],
                dst_ref=qall_ref.at[src, rows],
                send_sem=q_send.at[src, way, c],
                recv_sem=q_recv.at[src, c],
                device_id={"seq": dest},
                device_id_type=mesh_ids,
            )
        ]
        if c == 0:
            found.append(
                pltpu.make_async_remote_copy(
                    src_ref=hs_ref if first else hsall_ref.at[src],
                    dst_ref=hsall_ref.at[src],
                    send_sem=hs_send.at[src, way],
                    recv_sem=hs_recv.at[src],
                    device_id={"seq": dest},
                    device_id_type=mesh_ids,
                )
            )
        return found

    def send(src, c, first, way, dest):
        for copy in copies(src, c, first, way, dest):
            copy.start()

    def await_send(src, first, way, dest):
        for c in range(2):
            for copy in copies(src, c, first, way, dest):
                copy.wait_send()

    def await_recv(src, c):
        for copy in copies(src, c, False, 0, me):
            copy.wait_recv()

    for c in range(2):

        @pl.when(a > 0)
        def _():
            send(me, c, True, 0, me - minor)

        @pl.when(a < major - 1)
        def _():
            send(me, c, True, 1, me + minor)

        send(me, c, True, 2, mate)
    own_q = pltpu.make_async_copy(q_ref, qall_ref.at[me], own_sem.at[0])
    own_hs = pltpu.make_async_copy(hs_ref, hsall_ref.at[me], own_sem.at[1])
    own_q.start()
    own_hs.start()
    per_host, steps = nh_ref.shape[:2]
    for copy in small:
        copy.wait()
    nh_buf[...] = jnp.zeros_like(nh_buf)
    for i in range(per_host):
        nh_buf[i * steps : (i + 1) * steps, :] = nh_ref[i].astype(jnp.float32)
    down_copy.wait()
    raw_mine[...] = lax.dot_general(
        nh_buf[...].astype(jnp.bfloat16), down_buf[...], trans_b,
        preferred_element_type=jnp.float32,
    )
    raw_copy = pltpu.make_async_remote_copy(
        src_ref=raw_mine,
        dst_ref=raw_other,
        send_sem=raw_send,
        recv_sem=raw_recv,
        device_id={"head": 1 - head},
        device_id_type=mesh_ids,
    )
    raw_copy.start()

    def forward_down(d, c):
        src = me + d * minor

        @pl.when(a + d < major)
        def _():
            await_recv(src, c)

            @pl.when(a > 0)
            def _():
                send(src, c, False, 0, me - minor)

            send(src, c, False, 2, mate)

    def forward_up(d, c):
        src = me - d * minor

        @pl.when(a - d >= 0)
        def _():
            await_recv(src, c)

            @pl.when(a < major - 1)
            def _():
                send(src, c, False, 1, me + minor)

            send(src, c, False, 2, mate)

    def page_lists():
        prompts, table_width = table_ref.shape
        list_width = list_buf.shape[2]
        column = lax.broadcasted_iota(jnp.int32, (1, table_width), 1)
        earlier = lax.broadcasted_iota(jnp.int32, (table_width, table_width), 0)
        later = lax.broadcasted_iota(jnp.int32, (table_width, table_width), 1)
        before = jnp.where(earlier < later, 1.0, 0.0).astype(jnp.bfloat16)
        order = lax.broadcasted_iota(jnp.int32, (list_width, table_width), 0)
        line = lax.broadcasted_iota(jnp.int32, (8, table_width), 0)
        for p in range(prompts):
            local = table_ref[p : p + 1, :] - me * page_count
            owned = jnp.where(jnp.logical_and(local >= 0, local < page_count), 1, 0)
            many = jnp.broadcast_to(owned, (8, table_width)).astype(jnp.float32)
            rank = jnp.dot(
                many.astype(jnp.bfloat16), before, preferred_element_type=jnp.float32
            )[0:1].astype(jnp.int32)
            hot = jnp.where(jnp.logical_and(order == rank, owned > 0), 1.0, 0.0)
            left = jnp.minimum(len_ref[p] - column * page_rows, page_rows)
            count = jnp.sum(owned, axis=1, keepdims=True)
            values = jnp.where(line == 0, local * owned, left * owned).astype(jnp.float32)
            picked = lax.dot_general(
                values.astype(jnp.bfloat16), hot.astype(jnp.bfloat16), trans_b,
                preferred_element_type=jnp.float32,
            ).astype(jnp.int32)
            picked_line = lax.broadcasted_iota(jnp.int32, picked.shape, 0)
            list_buf[p] = jnp.where(picked_line == 2, count, picked)

    width = gain_ref.shape[1]
    extra = []
    for d in range(1, major):
        for c in range(2):
            forward_down(d, c)
            forward_up(d, c)
        if d == major - 1:
            raw_copy.wait()
            raw = raw_mine[...] + raw_other[...]
            latent = raw[:, :width]
            spread = lax.rsqrt(jnp.mean(latent * latent, axis=-1, keepdims=True) + eps)
            done = jnp.concatenate(
                [latent * spread * gain_ref[...], raw[:, width:]], axis=1
            )
            rows_buf[...] = jnp.concatenate([done, jnp.zeros_like(done)], axis=0).astype(
                jnp.bfloat16
            )
            for i in range(per_host):
                new_buf[i] = done[i * steps : (i + 1) * steps].astype(jnp.bfloat16)
            page_lists()
            extra = [
                pltpu.make_async_copy(rows_buf, rows_ref, own_sem.at[2]),
                pltpu.make_async_copy(list_buf, list_ref, own_sem.at[3]),
                pltpu.make_async_copy(new_buf, new_ref, own_sem.at[4]),
            ]
            for copy in extra:
                copy.start()
    for k in range(major):
        for c in range(2):
            await_recv(k * minor + (1 - b), c)
    own_q.wait()
    own_hs.wait()
    for copy in extra:
        copy.wait()
    for k in range(major):
        src = k * minor + b

        @pl.when(jnp.logical_and(a > 0, k >= a))
        def _():
            await_send(src, False, 0, me - minor)

        @pl.when(jnp.logical_and(a < major - 1, k <= a))
        def _():
            await_send(src, False, 1, me + minor)

        await_send(src, False, 2, mate)


def attend_kernel(
    list_ref, hs_ref, q_hbm, fresh_hbm, new_in, pool_ref, up_ref, o_ref, ml_ref, new_out,
    q_ref, fresh_ref, in_sem, kbuf, sbuf, sfresh, qp, acc, oacc, mbuf, lbuf, mlcol, upbuf, slot_of, page_sem, up_sem,
):
    prompts = list_ref.shape[0]
    per_host = 2
    slots, slot_rows, width = q_ref.shape
    heads, latent, vhead = up_ref.shape
    rows = fork_count * slot_rows
    me = lax.axis_index("seq")

    def page_copy(p, i, at):
        return pltpu.make_async_copy(pool_ref.at[list_ref[p, 0, i]], kbuf.at[at], page_sem.at[at])

    def blocks_of(p):
        return (list_ref[p, 2, 0] + block_pages - 1) // block_pages

    def start_prompt(p, base):
        count = blocks_of(p) * block_pages

        def start_page(i, carry):
            page_copy(p, i, base + i).start()
            return carry

        lax.fori_loop(0, count, start_page, 0)
        return base + count

    first = [
        pltpu.make_async_copy(q_hbm, q_ref, in_sem.at[0]),
        pltpu.make_async_copy(fresh_hbm, fresh_ref, in_sem.at[1]),
    ]
    for copy in first:
        copy.start()
    lax.fori_loop(0, prompts, start_prompt, 0)
    new_copy = pltpu.make_async_copy(new_in, new_out, in_sem.at[2])
    new_copy.start()
    up_copy = pltpu.make_async_copy(up_ref, upbuf, up_sem)
    up_copy.start()

    def note_slot(i, carry):
        slot_of[hs_ref[i // per_host, 0, i % per_host]] = i
        return carry

    lax.fori_loop(0, slots, note_slot, 0)
    for copy in first:
        copy.wait()
    lane = lax.broadcasted_iota(jnp.int32, (1, 128), 1)
    fresh_lane = lax.broadcasted_iota(jnp.int32, (slot_rows, 16), 1)
    step_of = lax.broadcasted_iota(jnp.int32, (slot_rows, 16), 0) // heads
    step_ok = jnp.logical_and(fresh_lane % 2 <= step_of, fresh_lane < 2 * per_host)

    def one_prompt(p, base):
        for f in range(fork_count):
            qp[f * slot_rows : (f + 1) * slot_rows, :] = q_ref[slot_of[p * fork_count + f]]
        fresh_all = (
            lax.dot_general(qp[...], fresh_ref[...], trans_b, preferred_element_type=jnp.float32)
            * log2_scale
        )
        for f in range(fork_count):
            part = slice(f * slot_rows, (f + 1) * slot_rows)
            mine = slot_of[p * fork_count + f] - me * per_host
            seen = jnp.logical_and(step_ok, fresh_lane // 2 == mine)
            scores = jnp.where(seen, fresh_all[part], floor_score)
            sfresh[part, :] = scores
            mbuf[part, :] = jnp.broadcast_to(
                jnp.max(scores, axis=1, keepdims=True), (slot_rows, 128)
            )
        blocks = blocks_of(p)

        def score_block(j, carry):
            for i in range(block_pages):
                page_copy(p, j * block_pages + i, base + j * block_pages + i).wait()
            keys = jnp.concatenate(
                [kbuf[base + j * block_pages + i] for i in range(block_pages)], axis=1
            )
            scores = jnp.dot(qp[...], keys, preferred_element_type=jnp.float32) * log2_scale
            top = mbuf[...]
            for i in range(block_pages):
                live = list_ref[p, 1, j * block_pages + i]
                piece = jnp.where(lane < live, scores[:, i * 128 : (i + 1) * 128], floor_score)
                sbuf[j, :, i * 128 : (i + 1) * 128] = piece
                top = jnp.maximum(top, piece)
            mbuf[...] = top
            return carry

        lax.fori_loop(0, blocks, score_block, 0)
        top = jnp.max(mbuf[...], axis=1, keepdims=True)
        mbuf[...] = jnp.broadcast_to(top, (rows, 128))
        fresh_scores = sfresh[...]
        fresh_w = jnp.where(fresh_scores > floor_score, jnp.exp2(fresh_scores - top), 0.0)
        fresh_total = jnp.sum(fresh_w, axis=1, keepdims=True)
        lbuf[...] = jnp.where(lane == 0, fresh_total, 0.0)
        fresh_w = fresh_w.astype(jnp.bfloat16)
        for c in range(latent // 128):
            acc[c] = jnp.dot(
                fresh_w, fresh_ref[:, c * 128 : (c + 1) * 128], preferred_element_type=jnp.float32
            )

        def add_block(j, carry):
            keys = jnp.concatenate(
                [kbuf[base + j * block_pages + i, :latent] for i in range(block_pages)], axis=1
            )
            top = mbuf[...]
            total = lbuf[...]
            rounded = []
            for i in range(block_pages):
                w = jnp.exp2(sbuf[j, :, i * 128 : (i + 1) * 128] - top)
                total = total + w
                rounded.append(w.astype(jnp.bfloat16))
            lbuf[...] = total
            part = lax.dot_general(
                jnp.concatenate(rounded, axis=1), keys, trans_b,
                preferred_element_type=jnp.float32,
            )
            for c in range(latent // 128):
                acc[c] += part[:, c * 128 : (c + 1) * 128]
            return carry

        lax.fori_loop(0, blocks, add_block, 0)
        total = jnp.sum(lbuf[...], axis=1, keepdims=True)
        ml = jnp.where(lane == 0, mbuf[...], total)

        @pl.when(p == 0)
        def _():
            up_copy.wait()

        group = 2 * fork_count
        for h in range(heads):
            x = jnp.concatenate(
                [acc[c, pl.ds(h, group, stride=heads), :] for c in range(latent // 128)], axis=1
            )
            hi = x.astype(jnp.bfloat16)
            lo = (x - hi.astype(jnp.float32)).astype(jnp.bfloat16)
            y = jnp.dot(
                jnp.concatenate([hi, lo], axis=0), upbuf[h], preferred_element_type=jnp.float32
            )
            oacc[pl.ds(h, group, stride=heads), :] = y[:group] + y[group:]
        for f in range(fork_count):
            part = slice(f * slot_rows, (f + 1) * slot_rows)
            slot = slot_of[p * fork_count + f]
            o_ref[slot] = oacc[part, :]
            mlcol[slot] = ml[part]
        return base + blocks * block_pages

    lax.fori_loop(0, prompts, one_prompt, 0)

    def turn(d, carry):
        both = mlcol[pl.ds(d * per_host, per_host)].reshape(per_host * slot_rows, 128)
        ml_ref[d] = both.T[0:8]
        return carry

    lax.fori_loop(0, slots // per_host, turn, 0)
    new_copy.wait()


def merge(blocks, ml_of, o_of, gains):
    top = ml_of(0)[0:1]
    for k in range(1, blocks):
        top = jnp.maximum(top, ml_of(k)[0:1])
    total = jnp.zeros_like(top)
    gains[...] = jnp.zeros_like(gains)
    for k in range(blocks):
        factor = jnp.exp2(ml_of(k)[0:1] - top)
        gains[k : k + 1, :] = factor
        total = total + factor * ml_of(k)[1:2]
    return top, total


def weigh(blocks, turned, o_of):
    out = turned[:, 0:1] * o_of(0)
    for k in range(1, blocks):
        out = out + turned[:, k : k + 1] * o_of(k)
    return out


def combine_kernel(
    n, o_ref, ml_ref, out_ref, o_own, ml_own, o_mate, ml_mate, o_pair, ml_pair, o_got, ml_got,
    gains, own_sem, mate_send, mate_recv, far_send, far_recv,
):
    minor = 2
    major = n // minor
    me = lax.axis_index("seq")
    a, b = me // minor, me % minor
    mate = a * minor + (1 - b)
    barrier = pltpu.get_barrier_semaphore()
    pl.semaphore_signal(barrier, inc=1, device_id={"seq": mate}, device_id_type=mesh_ids)
    for k in range(1, major):
        pl.semaphore_signal(
            barrier, inc=1, device_id={"seq": (me + k * minor) % n}, device_id_type=mesh_ids
        )
    order = list(range(1, major)) + [0]
    owns = []
    for k in order:
        place = (a + k) % major * minor + b
        pair = [
            pltpu.make_async_copy(ml_ref.at[place], ml_own.at[k], own_sem.at[k, 0]),
            pltpu.make_async_copy(o_ref.at[place], o_own.at[k], own_sem.at[k, 1]),
        ]
        for copy in pair:
            copy.start()
        owns.append(pair)
    pl.semaphore_wait(barrier, major)

    def push(src, dst, sems, k, i, dest):
        copy = pltpu.make_async_remote_copy(
            src_ref=src,
            dst_ref=dst,
            send_sem=sems[0].at[k, i],
            recv_sem=sems[1].at[k, i],
            device_id={"seq": dest},
            device_id_type=mesh_ids,
        )
        copy.start()
        return copy

    near = (mate_send, mate_recv)
    far = (far_send, far_recv)
    swaps = []
    for k in order:
        place = (a + k) % major * minor + (1 - b)
        swaps.append(
            [
                push(ml_ref.at[place], ml_mate.at[k], near, k, 0, mate),
                push(o_ref.at[place], o_mate.at[k], near, k, 1, mate),
            ]
        )
    sent = []
    line = lax.broadcasted_iota(jnp.int32, (8, 128), 0)
    for at, k in enumerate(order):
        for copy in owns[at]:
            copy.wait()
        for copy in swaps[at]:
            copy.wait_recv()
        ml_of = lambda i: (ml_own if i == 0 else ml_mate)[k]
        o_of = lambda i: (o_own if i == 0 else o_mate)[k]
        top, total = merge(2, ml_of, o_of, gains)
        summed = weigh(2, gains[...].T, o_of)
        both = jnp.where(line == 0, top, total)
        if k == 0:
            ml_got[0] = both
            o_got[0] = summed
        else:
            ml_pair[k] = both
            o_pair[k] = summed
            dest = (me + k * minor) % n
            sent.append(push(ml_pair.at[k], ml_got.at[k], far, k, 0, dest))
            sent.append(push(o_pair.at[k], o_got.at[k], far, k, 1, dest))
    for copy in sent:
        copy.wait_recv()
    top, total = merge(major, lambda i: ml_got[i], lambda i: o_got[i], gains)
    out = weigh(major, (gains[...] / total).T, lambda i: o_got[i])
    out_ref[...] = out.astype(jnp.bfloat16)
    for pair in swaps:
        for copy in pair:
            copy.wait_send()
    for copy in sent:
        copy.wait_send()


def attend(lists, hsall, qall, rows16, new_rows, pool, value_up):
    n = hsall.shape[0]
    prompts = lists.shape[0]
    slots, slot_rows, width = qall.shape
    heads, latent, vhead = value_up.shape
    page_count, page_rows = pool.shape[0], pool.shape[2]
    rows = fork_count * slot_rows
    score_blocks = -(-page_count // block_pages)
    slots_held = score_blocks * block_pages + (block_pages - 1) * prompts
    return pl.pallas_call(
        attend_kernel,
        out_shape=(
            jax.ShapeDtypeStruct((slots, slot_rows, vhead), jnp.float32),
            jax.ShapeDtypeStruct((n, 8, 128), jnp.float32),
            jax.ShapeDtypeStruct(new_rows.shape, jnp.bfloat16),
        ),
        in_specs=[smem, smem, hbm, hbm, hbm, hbm, hbm],
        out_specs=(vmem, vmem, hbm),
        scratch_shapes=[
            pltpu.VMEM((slots, slot_rows, width), jnp.bfloat16),
            pltpu.VMEM((16, width), jnp.bfloat16),
            pltpu.SemaphoreType.DMA((3,)),
            pltpu.VMEM((slots_held, width, page_rows), jnp.bfloat16),
            pltpu.VMEM((score_blocks, rows, block_pages * page_rows), jnp.float32),
            pltpu.VMEM((rows, 16), jnp.float32),
            pltpu.VMEM((rows, width), jnp.bfloat16),
            pltpu.VMEM((latent // 128, rows, 128), jnp.float32),
            pltpu.VMEM((rows, vhead), jnp.float32),
            pltpu.VMEM((rows, 128), jnp.float32),
            pltpu.VMEM((rows, 128), jnp.float32),
            pltpu.VMEM((slots, slot_rows, 128), jnp.float32),
            pltpu.VMEM(value_up.shape, jnp.bfloat16),
            pltpu.SMEM((slots,), jnp.int32),
            pltpu.SemaphoreType.DMA((slots_held,)),
            pltpu.SemaphoreType.DMA,
        ],
        compiler_params=pltpu.CompilerParams(vmem_limit_bytes=60 * 2**20),
    )(lists, hsall, qall, rows16, new_rows, pool, value_up)


def on_device(
    cache_pool, page_table, prompt_len, host_samples, queries, new_hidden, kv_down, kv_gain,
    value_up,
):
    n = lax.axis_size("seq")
    big = pltpu.CompilerParams
    per_host, steps, heads, width = queries.shape
    latent = kv_gain.shape[0]
    vhead = value_up.shape[2]
    page_count, page_rows = cache_pool.shape[:2]
    prompts = page_table.shape[0]
    host_rows = per_host * steps * heads
    slot_rows = steps * heads
    slots = n * per_host
    rows = fork_count * slot_rows
    list_width = -(-page_count // 128) * 128
    qall, hsall, rows16, new_rows, lists = pl.pallas_call(
        functools.partial(gather_kernel, n, page_count, page_rows),
        out_shape=(
            jax.ShapeDtypeStruct((n, host_rows, width), jnp.bfloat16),
            jax.ShapeDtypeStruct((n, 8, 128), jnp.int32),
            jax.ShapeDtypeStruct((16, width), jnp.bfloat16),
            jax.ShapeDtypeStruct((per_host, steps, width), jnp.bfloat16),
            jax.ShapeDtypeStruct((prompts, 8, list_width), jnp.int32),
        ),
        in_specs=[hbm, smem, hbm, hbm, hbm, hbm, smem],
        out_specs=(hbm, hbm, hbm, hbm, hbm),
        scratch_shapes=[
            pltpu.VMEM(kv_down.shape[::-1], jnp.bfloat16),
            pltpu.VMEM(new_hidden.shape, jnp.bfloat16),
            pltpu.VMEM((1, latent), jnp.float32),
            pltpu.VMEM(page_table.shape, jnp.int32),
            pltpu.VMEM((8, width), jnp.float32),
            pltpu.VMEM((8, width), jnp.float32),
            pltpu.VMEM((8, kv_down.shape[0]), jnp.float32),
            pltpu.VMEM((8, 128), jnp.int32),
            pltpu.VMEM((16, width), jnp.bfloat16),
            pltpu.VMEM((per_host, steps, width), jnp.bfloat16),
            pltpu.VMEM((prompts, 8, list_width), jnp.int32),
            pltpu.SemaphoreType.DMA,
            pltpu.SemaphoreType.DMA((8,)),
            pltpu.SemaphoreType.DMA((n, 3, 2)),
            pltpu.SemaphoreType.DMA((n, 2)),
            pltpu.SemaphoreType.DMA((n, 3)),
            pltpu.SemaphoreType.DMA((n,)),
            pltpu.SemaphoreType.DMA,
            pltpu.SemaphoreType.DMA,
        ],
        compiler_params=big(
            collective_id=0, has_side_effects=True, vmem_limit_bytes=62 * 2**20
        ),
    )(
        queries.reshape(host_rows, width), host_samples, new_hidden, kv_down.T, kv_gain[None, :],
        page_table, prompt_len,
    )

    o, ml, new_rows = attend(
        lists, hsall, qall.reshape(slots, slot_rows, width), rows16, new_rows,
        jnp.swapaxes(cache_pool, 1, 2), value_up,
    )

    out = pl.pallas_call(
        functools.partial(combine_kernel, n),
        out_shape=jax.ShapeDtypeStruct((host_rows, vhead), jnp.bfloat16),
        in_specs=[hbm, hbm],
        out_specs=vmem,
        scratch_shapes=[
            pltpu.VMEM((n // 2, lines, 128), jnp.float32)
            for _ in range(4)
            for lines in (host_rows, 8)
        ]
        + [
            pltpu.VMEM((128, 128), jnp.float32),
            pltpu.SemaphoreType.DMA((n // 2, 2)),
            pltpu.SemaphoreType.DMA((n // 2, 2)),
            pltpu.SemaphoreType.DMA((n // 2, 2)),
            pltpu.SemaphoreType.DMA((n // 2, 2)),
            pltpu.SemaphoreType.DMA((n // 2, 2)),
        ],
        compiler_params=big(
            collective_id=1, has_side_effects=True, vmem_limit_bytes=62 * 2**20
        ),
    )(o.reshape(n, host_rows, vhead), ml)
    return (new_rows, out.reshape(per_host, steps, heads, vhead))


def solution(mesh):
    in_specs = (
        P(("groups", "seq"), None, None),
        P("groups", None),
        P("groups"),
        P(("groups", "seq")),
        P(("groups", "seq"), None, "head", None),
        P(("groups", "seq"), None, "head"),
        P("head", None),
        P(),
        P("head", None, None),
    )
    out_specs = (P(("groups", "seq"), None, None), P(("groups", "seq"), None, "head", None))
    return jax.shard_map(
        on_device, mesh=mesh, in_specs=in_specs, out_specs=out_specs, check_vma=False
    )
```
